32 devices in a mesh: group: 2 (over y), dp: 4 (over x, core), tensor: 4 (over z).
Axes of the slice: x: 2, y: 2, z: 4, core: 2. Of those that a mesh axis runs over, the one named last changes fastest.
Arguments:
- x_feats: bfloat16 [4, 256, 8192], P(None, ('group', 'dp'), 'tensor'), parts along dimension 1, may hold values from -21 to 21, as said below
- w_query: bfloat16 [8192, 512], P(None, 'tensor'), may hold values from -0.0625 to 0.0625
- adapter_down: bfloat16 [64, 8192, 64], P(('group', 'dp'), 'tensor'), parts along dimension 0, may hold values from -0.0625 to 0.0625
- adapter_up: bfloat16 [64, 64, 512], P(('group', 'dp'), None, 'tensor'), parts along dimension 0, may hold values from -0.75 to 0.75
- agent_id: int32 [256], P(('group', 'dp')), parts along dimension 0, may hold values from 0 to 31, as said below
- adapter_slot: int32 [64], P('group'), parts along dimension 0, may hold values from 0 to 31, as said below
- cache_keys: bfloat16 [256, 192, 512], P(('group', 'dp', 'tensor')), parts along dimension 0, may hold values from -14 to 14, as said below
- cache_values: bfloat16 [256, 192, 512], P(('group', 'dp', 'tensor')), parts along dimension 0, may hold values from -6 to 6
- new_keys: bfloat16 [4, 256, 512], P(None, ('group', 'dp', 'tensor')), parts along dimension 1, may hold values from -6 to 6
- new_values: bfloat16 [4, 256, 512], P(None, ('group', 'dp', 'tensor')), parts along dimension 1, may hold values from -6 to 6
- lengths: int32 [256], P(('group', 'dp', 'tensor')), parts along dimension 0, may hold values from 1 to 192, as said below
Outputs:
- attended: bfloat16 [4, 256, 512], P(None, ('group', 'dp', 'tensor')), parts along dimension 1
The draws below stay inside these ranges and needn't reach their ends.
There are 2 independent parts, one for each index of `group`. The reference program is written for one: setup_inputs(seed, part) draws one part's arguments, and reference() takes and returns one part's arrays. A program takes and returns all parts, laid end to end along the dimension named above; an argument that names none is the same for every part. Nothing has to cross between parts.
Inputs may be any that keep to these rules, and one draw needn't show every extreme that they name: `x_feats`: a draw of bounded magnitude. `cache_keys`: a draw of bounded magnitude. A permutation; the adapter of persona a is stored on dp index adapter_slot[a] // 8. `agent_id`: among the rows of one dp index at most 8 have adapters stored on any one dp index; in every draw one dp index stores the adapters of exactly 8 rows of every dp index. `lengths`: every device's rows include one of length 192.
All inputs are finite; a program needn't handle non-finite values.
Results may differ from the reference program's by a relative error of at most 0.009.
The reference program's roundings to bfloat16 on the way count: a program that leaves them out, or rounds other values in their place, can miss the bound.
Values may be sent and summed in bfloat16 or wider, within the bound.
A program may use at most 128 MiB of HBM per device.

```python
import jax
import jax.numpy as jnp
from jax import lax

D = 8192
HD = 128
KVH = 4
RANK = 64
STEPS = 4
AG_DEV = 8
ROWS_DEV = 8
LMAX = 192
QH = 4
AGENTS = 32
DP_ROWS = 32
ROWS = 128
CAP = 8
N_DP = 4


def routing(key):
    key = jax.random.fold_in(key, 11)
    slot_key, hot_key, perm_key, shuffle_key, choose_key = jax.random.split(key, 5)
    slot_table = jax.random.permutation(slot_key, AGENTS).astype(jnp.int32)
    agent_at = jnp.zeros((AGENTS,), jnp.int32).at[slot_table].set(jnp.arange(AGENTS, dtype=jnp.int32))
    hot_home = jax.random.randint(hot_key, (), 0, N_DP)

    def one_source(source):
        slot_tags = jax.random.permutation(jax.random.fold_in(perm_key, source), N_DP * CAP).astype(jnp.int32)
        priority = jnp.where(slot_tags // CAP == hot_home, 0, 1)
        ordering = jnp.argsort(priority, stable=True)
        chosen_homes = slot_tags[ordering][:DP_ROWS] // CAP
        shuffle = jax.random.permutation(jax.random.fold_in(shuffle_key, source), DP_ROWS)
        return chosen_homes[shuffle]
    homes = jax.vmap(one_source)(jnp.arange(N_DP))
    local_pick = jax.random.randint(choose_key, (N_DP, DP_ROWS), 0, AG_DEV)
    agents = agent_at[homes * AG_DEV + local_pick].reshape(ROWS)
    return (agents.astype(jnp.int32), slot_table)


def draw_agent_id(key, part):
    return routing(key)[0]


def draw_adapter_slot(key, part):
    return routing(key)[1]


def draw_x_feats(key, part):
    key = jax.random.fold_in(key, 3)
    first_key = jax.random.fold_in(key, 0)
    return jnp.clip(jax.random.normal(first_key, (STEPS, ROWS, D), jnp.float32), -6.0, 6.0).astype(jnp.bfloat16)


def draw_cache_keys(key, part):
    key = jax.random.fold_in(key, 5)
    first_key = jax.random.fold_in(key, 0)
    return jnp.clip(jax.random.normal(first_key, (ROWS, LMAX, KVH * HD), jnp.float32), -6.0, 6.0).astype(jnp.bfloat16)


def draw_lengths(key, part):
    key = jax.random.fold_in(key, 7)
    first_key, second_key = jax.random.split(key)
    blocks = ROWS // ROWS_DEV
    drawn_lengths = jax.random.randint(first_key, (blocks, ROWS_DEV), 1, LMAX + 1)
    chosen_row = jax.random.randint(second_key, (blocks, 1), 0, ROWS_DEV)
    filled = jnp.where(jnp.arange(ROWS_DEV)[None, :] == chosen_row, LMAX, drawn_lengths)
    return filled.reshape(ROWS).astype(jnp.int32)


def levels(stream_key, extent, shards, low, high):
    def one(position, shards_of):
        heights = jax.random.uniform(jax.random.fold_in(jax.random.fold_in(stream_key, 6), position), (shards_of,), jnp.float32, low / len(shards), high / len(shards))
        return jnp.repeat(jnp.exp(heights), extent[position] // shards_of).reshape((-1,) + (1,) * (len(extent) - position - 1))

    loudness = one(*shards[0])
    for cut in shards[1:]:
        loudness = loudness * one(*cut)
    return loudness


def gaussian(stream_key, shape, spread, limit, cuts=(), held_as=jnp.bfloat16):
    loudness = levels(stream_key, shape, cuts, -0.22, 0.18) if cuts else 1.0
    result = jax.random.normal(stream_key, shape, jnp.float32) * spread * loudness
    return jnp.minimum(jnp.maximum(result, -limit), limit).astype(held_as)


def setup_inputs(seed: int = 0, part: int = 0) -> dict:
    key_of = jax.random.split(jax.random.key(seed), 12)
    part_keys = jax.random.split(jax.random.fold_in(key_of[11], part), 12)
    return {
        "x_feats": draw_x_feats(jax.random.fold_in(jax.random.fold_in(key_of[11], part), 71), part),
        "w_query": gaussian(key_of[1], (D, QH * HD), D ** -0.5, 0.0625, ((1, 4),)),
        "adapter_down": gaussian(part_keys[2], (AGENTS, D, RANK), D ** -0.5, 0.0625, ((0, 4), (1, 4))),
        "adapter_up": gaussian(part_keys[3], (AGENTS, RANK, QH * HD), RANK ** -0.5, 0.75, ((0, 4), (2, 4))),
        "agent_id": draw_agent_id(jax.random.fold_in(jax.random.fold_in(key_of[11], part), 71), part),
        "adapter_slot": draw_adapter_slot(jax.random.fold_in(jax.random.fold_in(key_of[11], part), 71), part),
        "cache_keys": draw_cache_keys(jax.random.fold_in(jax.random.fold_in(key_of[11], part), 71), part),
        "cache_values": gaussian(part_keys[7], (ROWS, LMAX, KVH * HD), 1.0, 6.0, ((0, 16),)),
        "new_keys": gaussian(part_keys[8], (STEPS, ROWS, KVH * HD), 1.0, 6.0, ((1, 16),)),
        "new_values": gaussian(part_keys[9], (STEPS, ROWS, KVH * HD), 1.0, 6.0, ((1, 16),)),
        "lengths": draw_lengths(jax.random.fold_in(jax.random.fold_in(key_of[11], part), 71), part),
    }


def attention(queries, key_cache, value_cache, fresh_keys, fresh_values, lengths):
    step_count, row_count, width = queries.shape
    group_size = width // (KVH * HD)
    length_max = key_cache.shape[1]
    score_scale = HD ** -0.5
    query_five = queries.astype(jnp.float32).reshape(step_count, row_count, KVH, group_size, HD)
    keys_four = key_cache.astype(jnp.float32).reshape(row_count, length_max, KVH, HD)
    values_four = value_cache.astype(jnp.float32).reshape(row_count, length_max, KVH, HD)
    fresh_four = fresh_keys.astype(jnp.float32).reshape(step_count, row_count, KVH, HD)
    fresh_vals = fresh_values.astype(jnp.float32).reshape(step_count, row_count, KVH, HD)
    old_scores = jnp.einsum('srgqd,rjgd->srgqj', query_five, keys_four) * score_scale
    new_scores = jnp.einsum('srgqd,trgd->srgqt', query_five, fresh_four) * score_scale
    valid_old = (jnp.arange(length_max)[None, :] < lengths[:, None])[None, :, None, None, :]
    valid_new = (jnp.arange(step_count)[None, :] <= jnp.arange(step_count)[:, None])[:, None, None, None, :]
    scores = jnp.concatenate([jnp.where(valid_old, old_scores, -jnp.inf), jnp.where(valid_new, new_scores, -jnp.inf)], axis=-1)
    weights = jax.nn.softmax(scores, axis=-1).astype(jnp.bfloat16)
    weights = lax.optimization_barrier(weights).astype(jnp.float32)
    mixed = jnp.einsum('srgqj,rjgd->srgqd', weights[..., :length_max], values_four)
    mixed = mixed + jnp.einsum('srgqt,trgd->srgqd', weights[..., length_max:], fresh_vals)
    return mixed.astype(jnp.bfloat16).reshape(step_count, row_count, width)


def reference(x_feats, w_query, adapter_down, adapter_up, agent_id, adapter_slot, cache_keys, cache_values, new_keys, new_values, lengths):
    step_count, row_count, width_model = x_feats.shape
    base = jnp.dot(x_feats.reshape(step_count * row_count, width_model), w_query, preferred_element_type=jnp.float32)
    base = base.reshape(step_count, row_count, -1)
    slot_ids = adapter_slot[agent_id].astype(jnp.int32)

    def adapt_row(pair):
        row_feats, slot_one = pair
        low_rank = jnp.dot(row_feats, adapter_down[slot_one], preferred_element_type=jnp.float32).astype(jnp.bfloat16)
        return jnp.dot(low_rank, adapter_up[slot_one], preferred_element_type=jnp.float32).astype(jnp.bfloat16)

    delta_rows = lax.map(adapt_row, (jnp.transpose(x_feats, (1, 0, 2)), slot_ids))
    delta_rows = lax.optimization_barrier(jnp.transpose(delta_rows, (1, 0, 2))).astype(jnp.float32)
    queries = (base + delta_rows).astype(jnp.bfloat16)
    queries = lax.optimization_barrier(queries)
    return attention(queries, cache_keys, cache_values, new_keys, new_values, lengths)
```

```python
import functools

import jax
import jax.numpy as jnp
from jax import lax
from jax.experimental import pallas as pl
from jax.experimental.pallas import tpu as pltpu
from jax.sharding import PartitionSpec as P

HD = 128
KVH = 4
MESH = pl.DeviceIdType.MESH
LANES = 128
VMEM_BYTES = 60 * 1024 * 1024


def attention(queries, key_cache, value_cache, fresh_keys, fresh_values, lengths):
    step_count, row_count, width = queries.shape
    group_size = width // (KVH * HD)
    length_max = key_cache.shape[1]
    score_scale = HD ** (-0.5)
    query_five = queries.reshape(step_count, row_count, KVH, group_size, HD)
    keys_four = key_cache.reshape(row_count, length_max, KVH, HD)
    values_four = value_cache.reshape(row_count, length_max, KVH, HD)
    fresh_four = fresh_keys.reshape(step_count, row_count, KVH, HD)
    fresh_vals = fresh_values.reshape(step_count, row_count, KVH, HD)
    old_scores = (
        jnp.einsum("srgqd,rjgd->srgqj", query_five, keys_four, preferred_element_type=jnp.float32)
        * score_scale
    )
    new_scores = (
        jnp.einsum("srgqd,trgd->srgqt", query_five, fresh_four, preferred_element_type=jnp.float32)
        * score_scale
    )
    valid_old = (jnp.arange(length_max)[None, :] < lengths[:, None])[None, :, None, None, :]
    valid_new = (jnp.arange(step_count)[None, :] <= jnp.arange(step_count)[:, None])[
        :, None, None, None, :
    ]
    scores = jnp.concatenate(
        [jnp.where(valid_old, old_scores, -jnp.inf), jnp.where(valid_new, new_scores, -jnp.inf)],
        axis=-1,
    )
    weights = jax.nn.softmax(scores, axis=-1).astype(jnp.bfloat16)
    mixed = jnp.einsum(
        "srgqj,rjgd->srgqd",
        weights[..., :length_max],
        values_four,
        preferred_element_type=jnp.float32,
    )
    mixed = mixed + jnp.einsum(
        "srgqt,trgd->srgqd",
        weights[..., length_max:],
        fresh_vals,
        preferred_element_type=jnp.float32,
    )
    return mixed.astype(jnp.bfloat16).reshape(step_count, row_count, width)


def rows_of(index, size):
    return pl.ds(pl.multiple_of(index * size, size), size)


def queries_kernel(
    sizes,
    x_ref,
    w_ref,
    down_ref,
    up_ref,
    agent_row_ref,
    agent_col_ref,
    slot_row_ref,
    slot_col_ref,
    out_ref,
    w_parts,
    down_buf,
    x_out,
    x_in,
    low_out,
    low_in,
    low_all,
    corr_out,
    corr_in,
    delta_out,
    delta_in,
    base_out,
    base_in,
    copy_sem,
    z_send,
    z_recv,
    d_send,
    d_recv,
    b_send,
    b_recv,
    c_send,
    c_recv,
    l_send,
    l_recv,
    a_send,
    a_recv,
    r_send,
    r_recv,
    e_send,
    e_recv,
    s_send,
    s_recv,
):
    n_group, n_dp, n_tensor, steps, rows, capacity, adapters, rank = sizes
    depth = w_parts.shape[1]
    n_chip_x = n_dp // 2
    chips = n_group * n_chip_x
    piece = depth // (2 * chips)
    row_block = rows // n_tensor
    per_home = steps * capacity
    items = n_dp * per_home
    low_rows = items // n_tensor

    group = lax.axis_index("group")
    dp = lax.axis_index("dp")
    tensor = lax.axis_index("tensor")
    core = lax.rem(dp, 2)
    chip = group * n_chip_x + dp // 2

    def at_chip(number, which):
        return (number // n_chip_x, lax.rem(number, n_chip_x) * 2 + which, tensor)

    sibling = (group, (dp // 2) * 2 + (1 - core), tensor)

    def remote(src, dst, send, recv, device):
        return pltpu.make_async_remote_copy(
            src_ref=src, dst_ref=dst, send_sem=send, recv_sem=recv, device_id=device,
            device_id_type=MESH,
        )

    def up_t(k):
        return lax.rem(tensor + k, n_tensor)

    def from_t(k):
        return lax.rem(tensor - k + n_tensor, n_tensor)

    def up_d(j):
        return lax.rem(dp + j, n_dp)

    def from_d(j):
        return lax.rem(dp - j + n_dp, n_dp)

    own_w = pltpu.make_async_copy(w_ref.at[rows_of(tensor, depth)], w_parts.at[0], copy_sem.at[0])
    own_down = pltpu.make_async_copy(down_ref, down_buf, copy_sem.at[1])
    own_w.start()
    own_down.start()

    barrier = pltpu.get_barrier_semaphore()
    for k in range(1, n_tensor):
        pl.semaphore_signal(barrier, inc=1, device_id=(group, dp, up_t(k)), device_id_type=MESH)
    for j in range(1, n_dp):
        pl.semaphore_signal(barrier, inc=1, device_id=(group, up_d(j), tensor), device_id_type=MESH)
    for other in range(1, n_group):
        for j in range(n_dp):
            if j % 2 == 0:
                pl.semaphore_signal(
                    barrier, inc=1,
                    device_id=(lax.rem(group + other, n_group), up_d(j), tensor),
                    device_id_type=MESH,
                )
    pl.semaphore_wait(barrier, n_tensor - 1 + n_dp - 1 + (n_group - 1) * n_chip_x)

    mine = rows_of(chip * 2 + core, piece)

    def z_copy(k):
        start = up_t(k) * depth + (chip * 2 + core) * piece
        return remote(
            w_ref.at[pl.ds(pl.multiple_of(start, piece), piece)], w_parts.at[k, mine],
            z_send.at[k], z_recv.at[k], (group, dp, up_t(k)),
        )

    lax.fori_loop(1, n_tensor, lambda k, c: (z_copy(k).start(), c)[1], 0)

    agents = slot_row_ref.shape[1]
    width = steps * rows
    slot_lane = jnp.sum(
        jnp.where(
            lax.broadcasted_iota(jnp.int32, (agents, width), 0) == agent_row_ref[...],
            slot_col_ref[...], 0,
        ),
        axis=0, keepdims=True,
    )
    slot_sub = jnp.sum(
        jnp.where(
            lax.broadcasted_iota(jnp.int32, (rows, agents), 1) == agent_col_ref[...],
            slot_row_ref[...], 0,
        ),
        axis=1, keepdims=True,
    )
    home_lane = slot_lane // adapters
    home_sub = slot_sub // adapters
    row_lane = lax.rem(lax.broadcasted_iota(jnp.int32, (rows, width), 1), rows)
    earlier = (home_sub == home_lane) & (
        lax.broadcasted_iota(jnp.int32, (rows, width), 0) < row_lane
    )
    place_lane = jnp.sum(earlier.astype(jnp.int32), axis=0, keepdims=True)
    step_lane = lax.broadcasted_iota(jnp.int32, (1, width), 1) // rows
    target = jnp.where(
        place_lane < capacity, (home_lane * steps + step_lane) * capacity + place_lane, items
    )
    dispatch = jnp.where(
        lax.broadcasted_iota(jnp.int32, (items, width), 0) == target, 1.0, 0.0
    )
    local_index = jnp.sum(dispatch * (slot_lane - home_lane * adapters).astype(jnp.float32),
                          axis=1, keepdims=True)
    dispatch = dispatch.astype(jnp.bfloat16)
    sent = jnp.dot(dispatch, x_ref[...], preferred_element_type=jnp.float32)
    x_out[:, :, :depth] = sent.astype(jnp.bfloat16).reshape(n_dp, per_home, depth)
    x_out[:, :, depth:] = jnp.broadcast_to(local_index, (items, LANES)).astype(
        jnp.bfloat16
    ).reshape(n_dp, per_home, LANES)

    d_copies = []
    for j in range(1, n_dp):
        d_copies.append(
            remote(x_out.at[up_d(j)], x_in.at[dp], d_send.at[j], d_recv.at[j],
                   (group, up_d(j), tensor))
        )
        d_copies[-1].start()
    x_in[dp] = x_out[dp]

    def b_copy(k, q):
        return remote(
            w_parts.at[k, mine], w_parts.at[k, mine], b_send.at[k, q], b_recv.at[k, q],
            at_chip(lax.rem(chip + q, chips), core),
        )

    def c_copy(k, q):
        part = rows_of(lax.rem(chip - q + chips, chips) * 2 + core, piece)
        return remote(
            w_parts.at[k, part], w_parts.at[k, part], c_send.at[k, q], c_recv.at[k, q], sibling
        )

    def b_arrival(k, q):
        part = rows_of(lax.rem(chip - q + chips, chips) * 2 + core, piece)
        return remote(
            w_parts.at[k, part], w_parts.at[k, part], b_send.at[k, q], b_recv.at[k, q],
            at_chip(lax.rem(chip + q, chips), core),
        )

    def c_arrival(k, q):
        part = rows_of(lax.rem(chip - q + chips, chips) * 2 + 1 - core, piece)
        return remote(
            w_parts.at[k, part], w_parts.at[k, part], c_send.at[k, q], c_recv.at[k, q], sibling
        )

    def spread(k, carry):
        z_copy(k).wait_recv()
        for q in range(1, chips):
            b_copy(k, q).start()
        c_copy(k, 0).start()
        return carry

    def forward(k, carry):
        for q in range(1, chips):
            b_arrival(k, q).wait_recv()
            c_copy(k, q).start()
        return carry

    cut = [1 + (n_tensor - 1) * i // 3 for i in range(4)]
    lax.fori_loop(1, n_tensor, spread, 0)

    own_down.wait()
    for copy in d_copies:
        copy.wait_recv()
    arrived = x_in[...].reshape(items, depth + LANES)
    chosen = arrived[:, depth:].astype(jnp.float32)[:, :rank]
    dense = lax.dot_general(
        arrived[:, :depth], down_buf[...], (((1,), (1,)), ((), ())),
        preferred_element_type=jnp.float32,
    )
    low = jnp.zeros((items, rank), jnp.float32)
    for a in range(adapters):
        low += jnp.where(chosen == float(a), dense[:, a * rank:(a + 1) * rank], 0.0)
    low_out[...] = low.reshape(n_tensor, low_rows, rank)
    l_copies = []
    for k in range(1, n_tensor):
        l_copies.append(
            remote(low_out.at[up_t(k)], low_in.at[k], l_send.at[k], l_recv.at[k],
                   (group, dp, up_t(k)))
        )
        l_copies[-1].start()
    lax.fori_loop(cut[0], cut[1], forward, 0)
    total = low_out[tensor]
    for k in range(1, n_tensor):
        l_copies[k - 1].wait_recv()
        total += low_in[k]
    low_all[tensor] = total.astype(jnp.bfloat16)
    a_copies = []
    for k in range(1, n_tensor):
        a_copies.append(
            remote(low_all.at[tensor], low_all.at[tensor], a_send.at[k], a_recv.at[k],
                   (group, dp, up_t(k)))
        )
        a_copies[-1].start()
    lax.fori_loop(cut[1], cut[2], forward, 0)
    for k in range(1, n_tensor):
        remote(low_all.at[from_t(k)], low_all.at[from_t(k)], a_send.at[k], a_recv.at[k],
               (group, dp, up_t(k))).wait_recv()
    low_rank = low_all[...].reshape(items, rank).astype(jnp.float32)
    spread_low = jnp.concatenate(
        [jnp.where(chosen == float(a), low_rank, 0.0) for a in range(adapters)], axis=1
    ).astype(jnp.bfloat16)
    corr = jnp.dot(spread_low, up_ref[...], preferred_element_type=jnp.float32)
    corr_out[...] = corr.astype(jnp.bfloat16).reshape(corr_out.shape)
    r_copies = []
    for j in range(1, n_dp):
        r_copies.append(
            remote(corr_out.at[up_d(j)], corr_in.at[dp], r_send.at[j], r_recv.at[j],
                   (group, up_d(j), tensor))
        )
        r_copies[-1].start()
    corr_in[dp] = corr_out[dp]
    lax.fori_loop(cut[2], cut[3], forward, 0)

    def project(k):
        block = jnp.dot(x_ref[...], w_parts[k], preferred_element_type=jnp.float32)
        column = from_t(k)
        for t in range(n_tensor):
            for s in range(steps):
                base_out[t, column, s * row_block:(s + 1) * row_block, :] = block[
                    s * rows + t * row_block:s * rows + (t + 1) * row_block
                ]
        for j in range(1, n_tensor):
            remote(base_out.at[up_t(j), column], base_in.at[j, column], s_send.at[j],
                   s_recv.at[j], (group, dp, up_t(j))).start()

    own_w.wait()
    project(0)

    for copy in r_copies:
        copy.wait_recv()
    delta = lax.dot_general(
        dispatch, corr_in[...].reshape(items, corr_in.shape[2]), (((0,), (0,)), ((), ())),
        preferred_element_type=jnp.float32,
    )
    for t in range(n_tensor):
        delta_out[t] = jnp.concatenate(
            [delta[s * rows + t * row_block:s * rows + (t + 1) * row_block] for s in range(steps)],
            axis=0,
        ).astype(jnp.bfloat16)
    e_copies = []
    for k in range(1, n_tensor):
        e_copies.append(
            remote(delta_out.at[up_t(k)], delta_in.at[tensor], e_send.at[k], e_recv.at[k],
                   (group, dp, up_t(k)))
        )
        e_copies[-1].start()
    delta_in[tensor] = delta_out[tensor]

    def project_arrived(k, carry):
        for q in range(chips):
            c_arrival(k, q).wait_recv()
        project(k)
        return carry

    lax.fori_loop(1, n_tensor, project_arrived, 0)

    for copy in e_copies:
        copy.wait_recv()
    base = base_out[tensor]
    s_waits = []
    for j in range(1, n_tensor):
        s_waits.append(
            remote(base_out.at[up_t(j)], base_in.at[j], s_send.at[j], s_recv.at[j],
                   (group, dp, up_t(j)))
        )
        s_waits[-1].wait_recv()
        base += base_in[j]
    out_ref[...] = (base + delta_in[...].astype(jnp.float32)).astype(jnp.bfloat16)

    for copy in d_copies + l_copies + a_copies + r_copies + e_copies + s_waits:
        copy.wait_send()

    def drain(k, carry):
        z_copy(k).wait_send()
        for q in range(1, chips):
            b_copy(k, q).wait_send()
        for q in range(chips):
            c_copy(k, q).wait_send()
        return carry

    lax.fori_loop(1, n_tensor, drain, 0)


def local(
    x_feats,
    w_query,
    adapter_down,
    adapter_up,
    agent_id,
    adapter_slot,
    cache_keys,
    cache_values,
    new_keys,
    new_values,
    lengths,
):
    steps, rows, depth = x_feats.shape
    columns = w_query.shape[1]
    n_group, n_dp, n_tensor = (lax.axis_size(name) for name in ("group", "dp", "tensor"))
    adapters, _, rank = adapter_down.shape
    capacity = rows // 4
    row_block = rows // n_tensor
    per_home = steps * capacity
    items = n_dp * per_home
    chips = n_group * n_dp // 2
    sizes = (n_group, n_dp, n_tensor, steps, rows, capacity, adapters, rank)
    vmem = pl.BlockSpec(memory_space=pltpu.VMEM)
    hbm = pl.BlockSpec(memory_space=pl.ANY)
    bf16, f32 = jnp.bfloat16, jnp.float32
    own = steps * row_block
    dma = pltpu.SemaphoreType.DMA
    tensor_sems = [dma((n_tensor,)), dma((n_tensor,))]
    dp_sems = [dma((n_dp,)), dma((n_dp,))]
    queries = pl.pallas_call(
        functools.partial(queries_kernel, sizes),
        out_shape=jax.ShapeDtypeStruct((n_tensor, own, columns), bf16),
        in_specs=[vmem, hbm, hbm, vmem, vmem, vmem, vmem, vmem],
        out_specs=vmem,
        scratch_shapes=[
            pltpu.VMEM((n_tensor, depth, columns), bf16),
            pltpu.VMEM((adapters * rank, depth), bf16),
            pltpu.VMEM((n_dp, per_home, depth + LANES), bf16),
            pltpu.VMEM((n_dp, per_home, depth + LANES), bf16),
            pltpu.VMEM((n_tensor, items // n_tensor, rank), f32),
            pltpu.VMEM((n_tensor, items // n_tensor, rank), f32),
            pltpu.VMEM((n_tensor, items // n_tensor, rank), bf16),
            pltpu.VMEM((n_dp, per_home, columns), bf16),
            pltpu.VMEM((n_dp, per_home, columns), bf16),
            pltpu.VMEM((n_tensor, own, columns), bf16),
            pltpu.VMEM((n_tensor, own, columns), bf16),
            pltpu.VMEM((n_tensor, n_tensor, own, columns), f32),
            pltpu.VMEM((n_tensor, n_tensor, own, columns), f32),
            dma((2,)),
            *tensor_sems,
            *dp_sems,
            dma((n_tensor, chips)),
            dma((n_tensor, chips)),
            dma((n_tensor, chips)),
            dma((n_tensor, chips)),
            *tensor_sems,
            *tensor_sems,
            *dp_sems,
            *tensor_sems,
            *tensor_sems,
        ],
        compiler_params=pltpu.CompilerParams(
            collective_id=0, has_side_effects=True, vmem_limit_bytes=VMEM_BYTES
        ),
        name="queries",
    )(
        x_feats.reshape(steps * rows, depth),
        w_query,
        jnp.swapaxes(adapter_down, 1, 2).reshape(adapters * rank, depth),
        adapter_up.reshape(adapters * rank, columns),
        jnp.tile(agent_id, steps).reshape(1, steps * rows),
        agent_id.reshape(rows, 1),
        adapter_slot.reshape(1, -1),
        adapter_slot.reshape(-1, 1),
    )
    row_queries = queries.reshape(n_tensor, steps, row_block, columns)
    row_queries = row_queries.transpose(1, 2, 0, 3).reshape(steps, row_block, n_tensor * columns)
    return attention(row_queries, cache_keys, cache_values, new_keys, new_values, lengths)


def solution(mesh):
    return jax.shard_map(
        local,
        mesh=mesh,
        in_specs=(
            P(None, ("group", "dp"), "tensor"),
            P(None, "tensor"),
            P(("group", "dp"), "tensor", None),
            P(("group", "dp"), None, "tensor"),
            P(("group", "dp")),
            P("group"),
            P(("group", "dp", "tensor"), None, None),
            P(("group", "dp", "tensor"), None, None),
            P(None, ("group", "dp", "tensor"), None),
            P(None, ("group", "dp", "tensor"), None),
            P(("group", "dp", "tensor")),
        ),
        out_specs=P(None, ("group", "dp", "tensor"), None),
        check_vma=False,
    )
```

```python
import functools

import jax
import jax.numpy as jnp
from jax import lax
from jax.experimental import pallas as pl
from jax.experimental.pallas import tpu as pltpu
from jax.sharding import PartitionSpec as P

HD = 128
KVH = 4
MESH = pl.DeviceIdType.MESH
LANES = 128
VMEM_BYTES = 60 * 1024 * 1024


def attend(steps, row_block, parts, keys_buf, values_buf, fresh_keys, fresh_values, lengths, out_ref):
    length_max = keys_buf.shape[1]
    cached = row_block * length_max
    queries = steps * row_block
    per_part = parts[0].shape[1] // HD
    group_size = len(parts) * per_part // KVH
    total = group_size * queries
    key_row = lax.broadcasted_iota(jnp.int32, (1, cached), 1) // length_max
    key_at = lax.rem(lax.broadcasted_iota(jnp.int32, (1, cached), 1), length_max)
    lane = lax.broadcasted_iota(jnp.int32, (1, row_block), 1)
    limit = jnp.zeros((1, cached), jnp.int32)
    for r in range(row_block):
        one = jnp.sum(jnp.where(lane == r, lengths, 0), axis=1, keepdims=True)
        limit = jnp.where(key_row == r, one, limit)
    key_row = jnp.where(key_at < limit, key_row, -1)
    query = lax.rem(lax.broadcasted_iota(jnp.int32, (total, 1), 0), queries)
    query_row, query_step = lax.rem(query, row_block), query // row_block
    old_valid = key_row == query_row
    fresh = lax.broadcasted_iota(jnp.int32, (1, queries), 1)
    new_valid = (lax.rem(fresh, row_block) == query_row) & (fresh // row_block <= query_step)
    contract = (((1,), (1,)), ((), ()))
    for g in range(KVH):
        cols = slice(g * HD, (g + 1) * HD)
        heads = range(g * group_size, (g + 1) * group_size)
        q = [parts[h // per_part][:, (h % per_part) * HD:(h % per_part + 1) * HD] for h in heads]
        q = (q[0] if len(q) == 1 else jnp.concatenate(q, axis=0)).astype(jnp.bfloat16)
        keys = keys_buf[:, :, cols].reshape(cached, HD)
        values = values_buf[:, :, cols].reshape(cached, HD)
        old = lax.dot_general(q, keys, contract, preferred_element_type=jnp.float32)
        new = lax.dot_general(
            q, fresh_keys[:, cols], contract, preferred_element_type=jnp.float32
        )
        old = jnp.where(old_valid, old * HD ** (-0.5), -jnp.inf)
        new = jnp.where(new_valid, new * HD ** (-0.5), -jnp.inf)
        top = jnp.maximum(
            jnp.max(old, axis=1, keepdims=True), jnp.max(new, axis=1, keepdims=True)
        )
        old, new = jnp.exp(old - top), jnp.exp(new - top)
        norm = jnp.sum(old, axis=1, keepdims=True) + jnp.sum(new, axis=1, keepdims=True)
        old, new = (old / norm).astype(jnp.bfloat16), (new / norm).astype(jnp.bfloat16)
        mixed = jnp.dot(old, values, preferred_element_type=jnp.float32)
        mixed += jnp.dot(new, fresh_values[:, cols], preferred_element_type=jnp.float32)
        for i, h in enumerate(heads):
            out_ref[:, :, h * HD:(h + 1) * HD] = (
                mixed[i * queries:(i + 1) * queries]
                .reshape(steps, row_block, HD)
                .astype(jnp.bfloat16)
            )


def rows_of(index, size):
    return pl.ds(pl.multiple_of(index * size, size), size)


def decode_kernel(
    sizes,
    x_ref,
    w_ref,
    down_ref,
    up_ref,
    agent_ref,
    slot_ref,
    keys_ref,
    values_ref,
    new_keys_ref,
    new_values_ref,
    lengths_ref,
    out_ref,
    w_parts,
    down_buf,
    x_out,
    x_in,
    low_out,
    low_in,
    low_all,
    corr_out,
    corr_in,
    delta_out,
    delta_in,
    base_out,
    base_in,
    keys_buf,
    values_buf,
    copy_sem,
    z_send,
    z_recv,
    d_send,
    d_recv,
    b_send,
    b_recv,
    c_send,
    c_recv,
    l_send,
    l_recv,
    a_send,
    a_recv,
    r_send,
    r_recv,
    e_send,
    e_recv,
    s_send,
    s_recv,
):
    n_group, n_dp, n_tensor, steps, rows, capacity, adapters, rank = sizes
    depth = w_parts.shape[1]
    n_chip_x = n_dp // 2
    chips = n_group * n_chip_x
    piece = depth // (2 * chips)
    row_block = rows // n_tensor
    per_home = steps * capacity
    items = n_dp * per_home
    low_rows = items // n_tensor

    group = lax.axis_index("group")
    dp = lax.axis_index("dp")
    tensor = lax.axis_index("tensor")
    core = lax.rem(dp, 2)
    chip = group * n_chip_x + dp // 2

    def at_chip(number, which):
        return (number // n_chip_x, lax.rem(number, n_chip_x) * 2 + which, tensor)

    sibling = (group, (dp // 2) * 2 + (1 - core), tensor)

    def remote(src, dst, send, recv, device):
        return pltpu.make_async_remote_copy(
            src_ref=src, dst_ref=dst, send_sem=send, recv_sem=recv, device_id=device,
            device_id_type=MESH,
        )

    def up_t(k):
        return lax.rem(tensor + k, n_tensor)

    def from_t(k):
        return lax.rem(tensor - k + n_tensor, n_tensor)

    def up_d(j):
        return lax.rem(dp + j, n_dp)

    def from_d(j):
        return lax.rem(dp - j + n_dp, n_dp)

    own_w = pltpu.make_async_copy(w_ref.at[rows_of(tensor, depth)], w_parts.at[0], copy_sem.at[0])
    own_down = pltpu.make_async_copy(down_ref, down_buf, copy_sem.at[1])
    own_w.start()
    own_down.start()
    own_keys = pltpu.make_async_copy(keys_ref, keys_buf, copy_sem.at[2])
    own_values = pltpu.make_async_copy(values_ref, values_buf, copy_sem.at[3])

    barrier = pltpu.get_barrier_semaphore()
    for k in range(1, n_tensor):
        pl.semaphore_signal(barrier, inc=1, device_id=(group, dp, up_t(k)), device_id_type=MESH)
    for j in range(1, n_dp):
        pl.semaphore_signal(barrier, inc=1, device_id=(group, up_d(j), tensor), device_id_type=MESH)
    for other in range(1, n_group):
        for j in range(n_dp):
            if j % 2 == 0:
                pl.semaphore_signal(
                    barrier, inc=1,
                    device_id=(lax.rem(group + other, n_group), up_d(j), tensor),
                    device_id_type=MESH,
                )
    pl.semaphore_wait(barrier, n_tensor - 1 + n_dp - 1 + (n_group - 1) * n_chip_x)

    mine = rows_of(chip * 2 + core, piece)

    def z_copy(k):
        start = up_t(k) * depth + (chip * 2 + core) * piece
        return remote(
            w_ref.at[pl.ds(pl.multiple_of(start, piece), piece)], w_parts.at[k, mine],
            z_send.at[k], z_recv.at[k], (group, dp, up_t(k)),
        )

    lax.fori_loop(1, n_tensor, lambda k, c: (z_copy(k).start(), c)[1], 0)

    agents = slot_ref.shape[1]
    width = steps * rows

    def as_column(row, count):
        diagonal = lax.broadcasted_iota(jnp.int32, (count, count), 0) == lax.broadcasted_iota(
            jnp.int32, (count, count), 1
        )
        return jnp.sum(jnp.where(diagonal, row, 0), axis=1, keepdims=True)

    agent_row, slot_row = agent_ref[...], slot_ref[...]
    agent_col, slot_col = as_column(agent_row, rows), as_column(slot_row, agents)
    agent_row = jnp.concatenate([agent_row] * steps, axis=1)
    slot_lane = jnp.sum(
        jnp.where(
            lax.broadcasted_iota(jnp.int32, (agents, width), 0) == agent_row,
            slot_col, 0,
        ),
        axis=0, keepdims=True,
    )
    slot_sub = jnp.sum(
        jnp.where(
            lax.broadcasted_iota(jnp.int32, (rows, agents), 1) == agent_col,
            slot_row, 0,
        ),
        axis=1, keepdims=True,
    )
    home_lane = slot_lane // adapters
    home_sub = slot_sub // adapters
    row_lane = lax.rem(lax.broadcasted_iota(jnp.int32, (rows, width), 1), rows)
    earlier = (home_sub == home_lane) & (
        lax.broadcasted_iota(jnp.int32, (rows, width), 0) < row_lane
    )
    place_lane = jnp.sum(earlier.astype(jnp.int32), axis=0, keepdims=True)
    step_lane = lax.broadcasted_iota(jnp.int32, (1, width), 1) // rows
    target = jnp.where(
        place_lane < capacity, (home_lane * steps + step_lane) * capacity + place_lane, items
    )
    dispatch = jnp.where(
        lax.broadcasted_iota(jnp.int32, (items, width), 0) == target, 1.0, 0.0
    )
    local_index = jnp.sum(dispatch * (slot_lane - home_lane * adapters).astype(jnp.float32),
                          axis=1, keepdims=True)
    dispatch = dispatch.astype(jnp.bfloat16)
    sent = jnp.dot(dispatch, x_ref[...], preferred_element_type=jnp.float32)
    x_out[:, :, :depth] = sent.astype(jnp.bfloat16).reshape(n_dp, per_home, depth)
    x_out[:, :, depth:] = jnp.broadcast_to(local_index, (items, LANES)).astype(
        jnp.bfloat16
    ).reshape(n_dp, per_home, LANES)

    d_copies = []
    for j in range(1, n_dp):
        d_copies.append(
            remote(x_out.at[up_d(j)], x_in.at[dp], d_send.at[j], d_recv.at[j],
                   (group, up_d(j), tensor))
        )
        d_copies[-1].start()
    x_in[dp] = x_out[dp]

    def b_copy(k, q):
        return remote(
            w_parts.at[k, mine], w_parts.at[k, mine], b_send.at[k, q], b_recv.at[k, q],
            at_chip(lax.rem(chip + q, chips), core),
        )

    def c_copy(k, q):
        part = rows_of(lax.rem(chip - q + chips, chips) * 2 + core, piece)
        return remote(
            w_parts.at[k, part], w_parts.at[k, part], c_send.at[k, q], c_recv.at[k, q], sibling
        )

    def b_arrival(k, q):
        part = rows_of(lax.rem(chip - q + chips, chips) * 2 + core, piece)
        return remote(
            w_parts.at[k, part], w_parts.at[k, part], b_send.at[k, q], b_recv.at[k, q],
            at_chip(lax.rem(chip + q, chips), core),
        )

    def c_arrival(k, q):
        part = rows_of(lax.rem(chip - q + chips, chips) * 2 + 1 - core, piece)
        return remote(
            w_parts.at[k, part], w_parts.at[k, part], c_send.at[k, q], c_recv.at[k, q], sibling
        )

    def spread(k, carry):
        z_copy(k).wait_recv()
        for q in range(1, chips):
            b_copy(k, q).start()
        c_copy(k, 0).start()
        return carry

    def forward(k, carry):
        for q in range(1, chips):
            b_arrival(k, q).wait_recv()
            c_copy(k, q).start()
        return carry

    cut = [1 + (n_tensor - 1) * i // 3 for i in range(4)]
    def project(k):
        block = jnp.dot(x_ref[...], w_parts[k], preferred_element_type=jnp.float32)
        column = from_t(k)
        for t in range(n_tensor):
            for s in range(steps):
                base_out[t, column, s * row_block:(s + 1) * row_block, :] = block[
                    s * rows + t * row_block:s * rows + (t + 1) * row_block
                ]
        for j in range(1, n_tensor):
            remote(base_out.at[up_t(j), column], base_in.at[j, column], s_send.at[j],
                   s_recv.at[j], (group, dp, up_t(j))).start()

    def project_arrived(k, carry):
        for q in range(chips):
            c_arrival(k, q).wait_recv()
        project(k)
        return carry

    own_w.wait()
    project(0)
    own_keys.start()
    own_values.start()
    lax.fori_loop(1, n_tensor, spread, 0)

    own_down.wait()
    for copy in d_copies:
        copy.wait_recv()
    arrived = x_in[...].reshape(items, depth + LANES)
    chosen = arrived[:, depth:].astype(jnp.float32)[:, :rank]
    dense = lax.dot_general(
        arrived[:, :depth], down_buf[...], (((1,), (1,)), ((), ())),
        preferred_element_type=jnp.float32,
    )
    low = jnp.zeros((items, rank), jnp.float32)
    for a in range(adapters):
        low += jnp.where(chosen == float(a), dense[:, a * rank:(a + 1) * rank], 0.0)
    low_out[...] = low.reshape(n_tensor, low_rows, rank)
    l_copies = []
    for k in range(1, n_tensor):
        l_copies.append(
            remote(low_out.at[up_t(k)], low_in.at[k], l_send.at[k], l_recv.at[k],
                   (group, dp, up_t(k)))
        )
        l_copies[-1].start()
    lax.fori_loop(cut[0], cut[1], forward, 0)
    total = low_out[tensor]
    for k in range(1, n_tensor):
        l_copies[k - 1].wait_recv()
        total += low_in[k]
    low_all[tensor] = total.astype(jnp.bfloat16)
    a_copies = []
    for k in range(1, n_tensor):
        a_copies.append(
            remote(low_all.at[tensor], low_all.at[tensor], a_send.at[k], a_recv.at[k],
                   (group, dp, up_t(k)))
        )
        a_copies[-1].start()
    lax.fori_loop(cut[1], cut[2], forward, 0)
    lax.fori_loop(cut[0], cut[1], project_arrived, 0)
    for k in range(1, n_tensor):
        remote(low_all.at[from_t(k)], low_all.at[from_t(k)], a_send.at[k], a_recv.at[k],
               (group, dp, up_t(k))).wait_recv()
    low_rank = low_all[...].reshape(items, rank).astype(jnp.float32)
    spread_low = jnp.concatenate(
        [jnp.where(chosen == float(a), low_rank, 0.0) for a in range(adapters)], axis=1
    ).astype(jnp.bfloat16)
    corr = jnp.dot(spread_low, up_ref[...], preferred_element_type=jnp.float32)
    corr_out[...] = corr.astype(jnp.bfloat16).reshape(corr_out.shape)
    r_copies = []
    for j in range(1, n_dp):
        r_copies.append(
            remote(corr_out.at[up_d(j)], corr_in.at[dp], r_send.at[j], r_recv.at[j],
                   (group, up_d(j), tensor))
        )
        r_copies[-1].start()
    corr_in[dp] = corr_out[dp]
    lax.fori_loop(cut[2], cut[3], forward, 0)
    lax.fori_loop(cut[1], cut[2], project_arrived, 0)


    for copy in r_copies:
        copy.wait_recv()
    delta = lax.dot_general(
        dispatch, corr_in[...].reshape(items, corr_in.shape[2]), (((0,), (0,)), ((), ())),
        preferred_element_type=jnp.float32,
    )
    for t in range(n_tensor):
        delta_out[t] = jnp.concatenate(
            [delta[s * rows + t * row_block:s * rows + (t + 1) * row_block] for s in range(steps)],
            axis=0,
        ).astype(jnp.bfloat16)
    e_copies = []
    for k in range(1, n_tensor):
        e_copies.append(
            remote(delta_out.at[up_t(k)], delta_in.at[tensor], e_send.at[k], e_recv.at[k],
                   (group, dp, up_t(k)))
        )
        e_copies[-1].start()
    delta_in[tensor] = delta_out[tensor]

    lax.fori_loop(cut[2], cut[3], project_arrived, 0)
    own_keys.wait()
    own_values.wait()

    for copy in e_copies:
        copy.wait_recv()
    base = base_out[tensor]
    s_waits = []
    for j in range(1, n_tensor):
        s_waits.append(
            remote(base_out.at[up_t(j)], base_in.at[j], s_send.at[j], s_recv.at[j],
                   (group, dp, up_t(j)))
        )
        s_waits[-1].wait_recv()
        base += base_in[j]
    parts = [base[t] + delta_in[t].astype(jnp.float32) for t in range(n_tensor)]
    fresh_shape = (steps * row_block, new_keys_ref.shape[2])
    attend(
        steps, row_block, parts, keys_buf, values_buf,
        new_keys_ref[...].astype(jnp.float32).reshape(fresh_shape).astype(jnp.bfloat16),
        new_values_ref[...].astype(jnp.float32).reshape(fresh_shape).astype(jnp.bfloat16),
        lengths_ref[...], out_ref,
    )

    for copy in d_copies + l_copies + a_copies + r_copies + e_copies + s_waits:
        copy.wait_send()

    def drain(k, carry):
        z_copy(k).wait_send()
        for q in range(1, chips):
            b_copy(k, q).wait_send()
        for q in range(chips):
            c_copy(k, q).wait_send()
        return carry

    lax.fori_loop(1, n_tensor, drain, 0)


def local(
    x_feats,
    w_query,
    adapter_down,
    adapter_up,
    agent_id,
    adapter_slot,
    cache_keys,
    cache_values,
    new_keys,
    new_values,
    lengths,
):
    steps, rows, depth = x_feats.shape
    columns = w_query.shape[1]
    n_group, n_dp, n_tensor = (lax.axis_size(name) for name in ("group", "dp", "tensor"))
    adapters, _, rank = adapter_down.shape
    capacity = rows // 4
    row_block = rows // n_tensor
    per_home = steps * capacity
    items = n_dp * per_home
    chips = n_group * n_dp // 2
    sizes = (n_group, n_dp, n_tensor, steps, rows, capacity, adapters, rank)
    vmem = pl.BlockSpec(memory_space=pltpu.VMEM)
    hbm = pl.BlockSpec(memory_space=pl.ANY)
    bf16, f32 = jnp.bfloat16, jnp.float32
    own = steps * row_block
    dma = pltpu.SemaphoreType.DMA
    tensor_sems = [dma((n_tensor,)), dma((n_tensor,))]
    dp_sems = [dma((n_dp,)), dma((n_dp,))]
    return pl.pallas_call(
        functools.partial(decode_kernel, sizes),
        out_shape=jax.ShapeDtypeStruct((steps, row_block, n_tensor * columns), bf16),
        in_specs=[vmem, hbm, hbm, vmem, vmem, vmem, hbm, hbm, vmem, vmem, vmem],
        out_specs=vmem,
        scratch_shapes=[
            pltpu.VMEM((n_tensor, depth, columns), bf16),
            pltpu.VMEM((adapters * rank, depth), bf16),
            pltpu.VMEM((n_dp, per_home, depth + LANES), bf16),
            pltpu.VMEM((n_dp, per_home, depth + LANES), bf16),
            pltpu.VMEM((n_tensor, items // n_tensor, rank), f32),
            pltpu.VMEM((n_tensor, items // n_tensor, rank), f32),
            pltpu.VMEM((n_tensor, items // n_tensor, rank), bf16),
            pltpu.VMEM((n_dp, per_home, columns), bf16),
            pltpu.VMEM((n_dp, per_home, columns), bf16),
            pltpu.VMEM((n_tensor, own, columns), bf16),
            pltpu.VMEM((n_tensor, own, columns), bf16),
            pltpu.VMEM((n_tensor, n_tensor, own, columns), f32),
            pltpu.VMEM((n_tensor, n_tensor, own, columns), f32),
            pltpu.VMEM(cache_keys.shape, bf16),
            pltpu.VMEM(cache_values.shape, bf16),
            dma((4,)),
            *tensor_sems,
            *dp_sems,
            dma((n_tensor, chips)),
            dma((n_tensor, chips)),
            dma((n_tensor, chips)),
            dma((n_tensor, chips)),
            *tensor_sems,
            *tensor_sems,
            *dp_sems,
            *tensor_sems,
            *tensor_sems,
        ],
        compiler_params=pltpu.CompilerParams(
            collective_id=0, has_side_effects=True, vmem_limit_bytes=VMEM_BYTES
        ),
        name="decode",
    )(
        x_feats.reshape(steps * rows, depth),
        w_query,
        jnp.swapaxes(adapter_down, 1, 2).reshape(adapters * rank, depth),
        adapter_up.reshape(adapters * rank, columns),
        agent_id.reshape(1, rows),
        adapter_slot.reshape(1, -1),
        cache_keys,
        cache_values,
        new_keys,
        new_values,
        lengths.reshape(1, -1),
    )


def solution(mesh):
    return jax.shard_map(
        local,
        mesh=mesh,
        in_specs=(
            P(None, ("group", "dp"), "tensor"),
            P(None, "tensor"),
            P(("group", "dp"), "tensor", None),
            P(("group", "dp"), None, "tensor"),
            P(("group", "dp")),
            P("group"),
            P(("group", "dp", "tensor"), None, None),
            P(("group", "dp", "tensor"), None, None),
            P(None, ("group", "dp", "tensor"), None),
            P(None, ("group", "dp", "tensor"), None),
            P(("group", "dp", "tensor")),
        ),
        out_specs=P(None, ("group", "dp", "tensor"), None),
        check_vma=False,
    )
```

```python
import functools

import jax
import jax.numpy as jnp
from jax import lax
from jax.experimental import pallas as pl
from jax.experimental.pallas import tpu as pltpu
from jax.sharding import PartitionSpec as P

HD = 128
KVH = 4
MESH = pl.DeviceIdType.MESH
LANES = 128
VMEM_BYTES = 62 * 1024 * 1024


def attend(steps, row_block, parts, keys_buf, values_buf, fresh_keys, fresh_values, lengths, out_ref):
    length_max = keys_buf.shape[1]
    cached = row_block * length_max
    queries = steps * row_block
    per_part = parts[0].shape[1] // HD
    group_size = len(parts) * per_part // KVH
    total = group_size * queries
    key_row = lax.broadcasted_iota(jnp.int32, (1, cached), 1) // length_max
    key_at = lax.rem(lax.broadcasted_iota(jnp.int32, (1, cached), 1), length_max)
    lane = lax.broadcasted_iota(jnp.int32, (1, row_block), 1)
    limit = jnp.zeros((1, cached), jnp.int32)
    for r in range(row_block):
        one = jnp.sum(jnp.where(lane == r, lengths, 0), axis=1, keepdims=True)
        limit = jnp.where(key_row == r, one, limit)
    key_row = jnp.where(key_at < limit, key_row, -1)
    query = lax.rem(lax.broadcasted_iota(jnp.int32, (total, 1), 0), queries)
    query_row, query_step = lax.rem(query, row_block), query // row_block
    old_valid = key_row == query_row
    fresh = lax.broadcasted_iota(jnp.int32, (1, queries), 1)
    new_valid = (lax.rem(fresh, row_block) == query_row) & (fresh // row_block <= query_step)
    contract = (((1,), (1,)), ((), ()))
    for g in range(KVH):
        cols = slice(g * HD, (g + 1) * HD)
        heads = range(g * group_size, (g + 1) * group_size)
        q = [parts[h // per_part][:, (h % per_part) * HD:(h % per_part + 1) * HD] for h in heads]
        q = (q[0] if len(q) == 1 else jnp.concatenate(q, axis=0)).astype(jnp.bfloat16)
        keys = keys_buf[:, :, cols].reshape(cached, HD)
        values = values_buf[:, :, cols].reshape(cached, HD)
        old = lax.dot_general(q, keys, contract, preferred_element_type=jnp.float32)
        new = lax.dot_general(
            q, fresh_keys[:, cols], contract, preferred_element_type=jnp.float32
        )
        old = jnp.where(old_valid, old * HD ** (-0.5), -jnp.inf)
        new = jnp.where(new_valid, new * HD ** (-0.5), -jnp.inf)
        top = jnp.maximum(
            jnp.max(old, axis=1, keepdims=True), jnp.max(new, axis=1, keepdims=True)
        )
        old, new = jnp.exp(old - top), jnp.exp(new - top)
        norm = jnp.sum(old, axis=1, keepdims=True) + jnp.sum(new, axis=1, keepdims=True)
        old, new = (old / norm).astype(jnp.bfloat16), (new / norm).astype(jnp.bfloat16)
        mixed = jnp.dot(old, values, preferred_element_type=jnp.float32)
        mixed += jnp.dot(new, fresh_values[:, cols], preferred_element_type=jnp.float32)
        for i, h in enumerate(heads):
            out_ref[:, :, h * HD:(h + 1) * HD] = (
                mixed[i * queries:(i + 1) * queries]
                .reshape(steps, row_block, HD)
            )


def rows_of(index, size):
    return pl.ds(pl.multiple_of(index * size, size), size)


def decode_kernel(
    sizes,
    x_ref,
    w_ref,
    down_ref,
    up_ref,
    agent_ref,
    slot_ref,
    keys_ref,
    values_ref,
    new_keys_ref,
    new_values_ref,
    lengths_ref,
    out_ref,
    w_parts,
    down_buf,
    x_out,
    x_in,
    low_out,
    low_in,
    low_all,
    corr_out,
    corr_in,
    delta_out,
    delta_in,
    base_out,
    base_in,
    keys_buf,
    values_buf,
    copy_sem,
    z_send,
    z_recv,
    d_send,
    d_recv,
    b_send,
    b_recv,
    c_send,
    c_recv,
    l_send,
    l_recv,
    a_send,
    a_recv,
    r_send,
    r_recv,
    e_send,
    e_recv,
    s_send,
    s_recv,
):
    n_group, n_dp, n_tensor, steps, rows, capacity, adapters, rank = sizes
    depth = w_parts.shape[1]
    n_chip_x = n_dp // 2
    chips = n_group * n_chip_x
    piece = depth // (2 * chips)
    row_block = rows // n_tensor
    per_home = steps * capacity
    items = n_dp * per_home
    low_rows = items // n_tensor

    group = lax.axis_index("group")
    dp = lax.axis_index("dp")
    tensor = lax.axis_index("tensor")
    core = lax.rem(dp, 2)
    chip = group * n_chip_x + dp // 2

    chip_x = dp // 2

    def part_of(q, which):
        g = lax.rem(group - q // n_chip_x + n_group, n_group)
        x = lax.rem(chip_x - q % n_chip_x + n_chip_x, n_chip_x)
        return rows_of((g * n_chip_x + x) * 2 + which, piece)

    sibling = (group, (dp // 2) * 2 + (1 - core), tensor)

    def remote(src, dst, send, recv, device):
        return pltpu.make_async_remote_copy(
            src_ref=src, dst_ref=dst, send_sem=send, recv_sem=recv, device_id=device,
            device_id_type=MESH,
        )

    def up_t(k):
        return lax.rem(tensor + k, n_tensor)

    def from_t(k):
        return lax.rem(tensor - k + n_tensor, n_tensor)

    def up_d(j):
        return lax.rem(dp + j, n_dp)

    def from_d(j):
        return lax.rem(dp - j + n_dp, n_dp)

    own_w = pltpu.make_async_copy(w_ref.at[rows_of(tensor, depth)], w_parts.at[0], copy_sem.at[0])
    own_down = pltpu.make_async_copy(down_ref, down_buf, copy_sem.at[1])
    own_w.start()
    own_down.start()
    own_keys = pltpu.make_async_copy(keys_ref, keys_buf, copy_sem.at[2])
    own_values = pltpu.make_async_copy(values_ref, values_buf, copy_sem.at[3])

    barrier = pltpu.get_barrier_semaphore()
    for k in range(1, n_tensor):
        pl.semaphore_signal(barrier, inc=1, device_id=(group, dp, up_t(k)), device_id_type=MESH)
    for j in range(1, n_dp):
        pl.semaphore_signal(barrier, inc=1, device_id=(group, up_d(j), tensor), device_id_type=MESH)
    for other in range(1, n_group):
        pl.semaphore_signal(
            barrier, inc=1, device_id=(lax.rem(group + other, n_group), dp, tensor),
            device_id_type=MESH,
        )
    pl.semaphore_wait(barrier, n_tensor - 1 + n_dp - 1 + n_group - 1)

    mine = rows_of(chip * 2 + core, piece)

    def z_copy(k):
        start = up_t(k) * depth + (chip * 2 + core) * piece
        return remote(
            w_ref.at[pl.ds(pl.multiple_of(start, piece), piece)], w_parts.at[k, mine],
            z_send.at[k], z_recv.at[k], (group, dp, up_t(k)),
        )

    lax.fori_loop(1, n_tensor, lambda k, c: (z_copy(k).start(), c)[1], 0)

    agents = slot_ref.shape[1]
    width = steps * rows

    def as_column(row, count):
        diagonal = lax.broadcasted_iota(jnp.int32, (count, count), 0) == lax.broadcasted_iota(
            jnp.int32, (count, count), 1
        )
        return jnp.sum(jnp.where(diagonal, row, 0), axis=1, keepdims=True)

    agent_row, slot_row = agent_ref[...], slot_ref[...]
    agent_col, slot_col = as_column(agent_row, rows), as_column(slot_row, agents)
    agent_row = jnp.concatenate([agent_row] * steps, axis=1)
    slot_lane = jnp.sum(
        jnp.where(
            lax.broadcasted_iota(jnp.int32, (agents, width), 0) == agent_row,
            slot_col, 0,
        ),
        axis=0, keepdims=True,
    )
    slot_sub = jnp.sum(
        jnp.where(
            lax.broadcasted_iota(jnp.int32, (rows, agents), 1) == agent_col,
            slot_row, 0,
        ),
        axis=1, keepdims=True,
    )
    home_lane = slot_lane // adapters
    home_sub = slot_sub // adapters
    row_lane = lax.rem(lax.broadcasted_iota(jnp.int32, (rows, width), 1), rows)
    earlier = (home_sub == home_lane) & (
        lax.broadcasted_iota(jnp.int32, (rows, width), 0) < row_lane
    )
    place_lane = jnp.sum(earlier.astype(jnp.int32), axis=0, keepdims=True)
    step_lane = lax.broadcasted_iota(jnp.int32, (1, width), 1) // rows
    target = jnp.where(
        place_lane < capacity, (home_lane * steps + step_lane) * capacity + place_lane, items
    )
    dispatch = jnp.where(
        lax.broadcasted_iota(jnp.int32, (items, width), 0) == target, 1.0, 0.0
    )
    local_index = jnp.sum(dispatch * (slot_lane - home_lane * adapters).astype(jnp.float32),
                          axis=1, keepdims=True)
    dispatch = dispatch.astype(jnp.bfloat16)
    sent = jnp.dot(dispatch, x_ref[...], preferred_element_type=jnp.float32)
    x_out[:, :, :depth] = sent.astype(jnp.bfloat16).reshape(n_dp, per_home, depth)
    x_out[:, :, depth:] = jnp.broadcast_to(local_index, (items, LANES)).astype(
        jnp.bfloat16
    ).reshape(n_dp, per_home, LANES)

    d_copies = []
    for j in range(1, n_dp):
        d_copies.append(
            remote(x_out.at[up_d(j)], x_in.at[dp], d_send.at[j], d_recv.at[j],
                   (group, up_d(j), tensor))
        )
        d_copies[-1].start()
    x_in[dp] = x_out[dp]

    def b_copy(k, q):
        back_group, back_x = q // n_chip_x, q % n_chip_x
        if back_group == 0:
            part = part_of(0, core)
            device = (group, lax.rem(chip_x + back_x, n_chip_x) * 2 + core, tensor)
        else:
            part = part_of(back_x, core)
            device = (lax.rem(group + back_group, n_group), dp, tensor)
        return remote(
            w_parts.at[k, part], w_parts.at[k, part], b_send.at[k, q], b_recv.at[k, q], device
        )

    def b_arrival(k, q):
        part = part_of(q, core)
        return remote(
            w_parts.at[k, part], w_parts.at[k, part], b_send.at[k, q], b_recv.at[k, q], sibling
        )

    def c_copy(k, q):
        part = part_of(q, core)
        return remote(
            w_parts.at[k, part], w_parts.at[k, part], c_send.at[k, q], c_recv.at[k, q], sibling
        )

    def c_arrival(k, q):
        part = part_of(q, 1 - core)
        return remote(
            w_parts.at[k, part], w_parts.at[k, part], c_send.at[k, q], c_recv.at[k, q], sibling
        )

    def spread(k, carry):
        z_copy(k).wait_recv()
        for j in range(1, n_chip_x):
            b_copy(k, j).start()
        for other in range(1, n_group):
            b_copy(k, other * n_chip_x).start()
        c_copy(k, 0).start()
        return carry

    def forward(k, carry):
        for j in range(1, n_chip_x):
            b_arrival(k, j).wait_recv()
            for other in range(1, n_group):
                b_copy(k, other * n_chip_x + j).start()
            c_copy(k, j).start()
        return carry

    def hand_over(k, carry):
        for q in range(n_chip_x, chips):
            b_arrival(k, q).wait_recv()
            c_copy(k, q).start()
        return carry

    cut = [1 + (n_tensor - 1) * i // 3 for i in range(4)]
    def project(k):
        block = jnp.dot(x_ref[...], w_parts[k], preferred_element_type=jnp.float32)
        column = from_t(k)
        for t in range(n_tensor):
            for s in range(steps):
                base_out[t, column, s * row_block:(s + 1) * row_block, :] = block[
                    s * rows + t * row_block:s * rows + (t + 1) * row_block
                ]
        for j in range(1, n_tensor):
            remote(base_out.at[up_t(j), column], base_in.at[j, column], s_send.at[j],
                   s_recv.at[j], (group, dp, up_t(j))).start()

    def project_arrived(k, carry):
        for q in range(chips):
            c_arrival(k, q).wait_recv()
        project(k)
        return carry

    own_w.wait()
    project(0)
    own_keys.start()
    own_values.start()
    lax.fori_loop(1, n_tensor, spread, 0)

    own_down.wait()
    for copy in d_copies:
        copy.wait_recv()
    arrived = x_in[...].reshape(items, depth + LANES)
    chosen = arrived[:, depth:].astype(jnp.float32)[:, :rank]
    dense = lax.dot_general(
        arrived[:, :depth], down_buf[...], (((1,), (1,)), ((), ())),
        preferred_element_type=jnp.float32,
    )
    low = jnp.zeros((items, rank), jnp.float32)
    for a in range(adapters):
        low += jnp.where(chosen == float(a), dense[:, a * rank:(a + 1) * rank], 0.0)
    low_out[...] = low.reshape(n_tensor, low_rows, rank)
    l_copies = []
    for k in range(1, n_tensor):
        l_copies.append(
            remote(low_out.at[up_t(k)], low_in.at[k], l_send.at[k], l_recv.at[k],
                   (group, dp, up_t(k)))
        )
        l_copies[-1].start()
    lax.fori_loop(cut[0], cut[1], forward, 0)
    total = low_out[tensor]
    for k in range(1, n_tensor):
        l_copies[k - 1].wait_recv()
        total += low_in[k]
    low_all[tensor] = total.astype(jnp.bfloat16)
    a_copies = []
    for k in range(1, n_tensor):
        a_copies.append(
            remote(low_all.at[tensor], low_all.at[tensor], a_send.at[k], a_recv.at[k],
                   (group, dp, up_t(k)))
        )
        a_copies[-1].start()
    lax.fori_loop(cut[1], cut[2], forward, 0)
    lax.fori_loop(cut[0], cut[1], hand_over, 0)
    for k in range(1, n_tensor):
        remote(low_all.at[from_t(k)], low_all.at[from_t(k)], a_send.at[k], a_recv.at[k],
               (group, dp, up_t(k))).wait_recv()
    low_rank = low_all[...].reshape(items, rank).astype(jnp.float32)
    spread_low = jnp.concatenate(
        [jnp.where(chosen == float(a), low_rank, 0.0) for a in range(adapters)], axis=1
    ).astype(jnp.bfloat16)
    corr = jnp.dot(spread_low, up_ref[...], preferred_element_type=jnp.float32)
    corr_out[...] = corr.astype(jnp.bfloat16).reshape(corr_out.shape)
    r_copies = []
    for j in range(1, n_dp):
        r_copies.append(
            remote(corr_out.at[up_d(j)], corr_in.at[dp], r_send.at[j], r_recv.at[j],
                   (group, up_d(j), tensor))
        )
        r_copies[-1].start()
    corr_in[dp] = corr_out[dp]
    lax.fori_loop(cut[2], cut[3], forward, 0)
    lax.fori_loop(cut[1], cut[2], hand_over, 0)
    lax.fori_loop(cut[0], cut[1], project_arrived, 0)


    for copy in r_copies:
        copy.wait_recv()
    delta = lax.dot_general(
        dispatch, corr_in[...].reshape(items, corr_in.shape[2]), (((0,), (0,)), ((), ())),
        preferred_element_type=jnp.float32,
    )
    for t in range(n_tensor):
        delta_out[t] = jnp.concatenate(
            [delta[s * rows + t * row_block:s * rows + (t + 1) * row_block] for s in range(steps)],
            axis=0,
        ).astype(jnp.bfloat16)
    e_copies = []
    for k in range(1, n_tensor):
        e_copies.append(
            remote(delta_out.at[up_t(k)], delta_in.at[tensor], e_send.at[k], e_recv.at[k],
                   (group, dp, up_t(k)))
        )
        e_copies[-1].start()
    delta_in[tensor] = delta_out[tensor]

    lax.fori_loop(cut[2], cut[3], hand_over, 0)
    lax.fori_loop(cut[1], cut[3], project_arrived, 0)
    own_keys.wait()
    own_values.wait()

    for copy in e_copies:
        copy.wait_recv()
    base = base_out[tensor]
    s_waits = []
    for j in range(1, n_tensor):
        s_waits.append(
            remote(base_out.at[up_t(j)], base_in.at[j], s_send.at[j], s_recv.at[j],
                   (group, dp, up_t(j)))
        )
        s_waits[-1].wait_recv()
        base += base_in[j]
    parts = [base[t] + delta_in[t].astype(jnp.float32) for t in range(n_tensor)]
    fresh_shape = (steps * row_block, new_keys_ref.shape[2])
    attend(
        steps, row_block, parts, keys_buf, values_buf,
        new_keys_ref[...].astype(jnp.float32).reshape(fresh_shape).astype(jnp.bfloat16),
        new_values_ref[...].astype(jnp.float32).reshape(fresh_shape).astype(jnp.bfloat16),
        lengths_ref[...], out_ref,
    )

    for copy in d_copies + l_copies + a_copies + r_copies + e_copies + s_waits:
        copy.wait_send()

    def drain(k, carry):
        z_copy(k).wait_send()
        for q in range(1, chips):
            b_copy(k, q).wait_send()
        for q in range(chips):
            c_copy(k, q).wait_send()
        return carry

    lax.fori_loop(1, n_tensor, drain, 0)


def local(
    x_feats,
    w_query,
    adapter_down,
    adapter_up,
    agent_id,
    adapter_slot,
    cache_keys,
    cache_values,
    new_keys,
    new_values,
    lengths,
):
    steps, rows, depth = x_feats.shape
    columns = w_query.shape[1]
    n_group, n_dp, n_tensor = (lax.axis_size(name) for name in ("group", "dp", "tensor"))
    adapters, _, rank = adapter_down.shape
    capacity = rows // 4
    row_block = rows // n_tensor
    per_home = steps * capacity
    items = n_dp * per_home
    chips = n_group * n_dp // 2
    sizes = (n_group, n_dp, n_tensor, steps, rows, capacity, adapters, rank)
    vmem = pl.BlockSpec(memory_space=pltpu.VMEM)
    hbm = pl.BlockSpec(memory_space=pl.ANY)
    bf16, f32 = jnp.bfloat16, jnp.float32
    own = steps * row_block
    dma = pltpu.SemaphoreType.DMA
    tensor_sems = [dma((n_tensor,)), dma((n_tensor,))]
    dp_sems = [dma((n_dp,)), dma((n_dp,))]
    return pl.pallas_call(
        functools.partial(decode_kernel, sizes),
        out_shape=jax.ShapeDtypeStruct((steps, row_block, n_tensor * columns), f32),
        in_specs=[vmem, hbm, hbm, vmem, vmem, vmem, hbm, hbm, vmem, vmem, vmem],
        out_specs=vmem,
        scratch_shapes=[
            pltpu.VMEM((n_tensor, depth, columns), bf16),
            pltpu.VMEM((adapters * rank, depth), bf16),
            pltpu.VMEM((n_dp, per_home, depth + LANES), bf16),
            pltpu.VMEM((n_dp, per_home, depth + LANES), bf16),
            pltpu.VMEM((n_tensor, items // n_tensor, rank), f32),
            pltpu.VMEM((n_tensor, items // n_tensor, rank), f32),
            pltpu.VMEM((n_tensor, items // n_tensor, rank), bf16),
            pltpu.VMEM((n_dp, per_home, columns), bf16),
            pltpu.VMEM((n_dp, per_home, columns), bf16),
            pltpu.VMEM((n_tensor, own, columns), bf16),
            pltpu.VMEM((n_tensor, own, columns), bf16),
            pltpu.VMEM((n_tensor, n_tensor, own, columns), f32),
            pltpu.VMEM((n_tensor, n_tensor, own, columns), f32),
            pltpu.VMEM(cache_keys.shape, bf16),
            pltpu.VMEM(cache_values.shape, bf16),
            dma((4,)),
            *tensor_sems,
            *dp_sems,
            dma((n_tensor, chips)),
            dma((n_tensor, chips)),
            dma((n_tensor, chips)),
            dma((n_tensor, chips)),
            *tensor_sems,
            *tensor_sems,
            *dp_sems,
            *tensor_sems,
            *tensor_sems,
        ],
        compiler_params=pltpu.CompilerParams(
            collective_id=0, has_side_effects=True, vmem_limit_bytes=VMEM_BYTES
        ),
        name="decode",
    )(
        x_feats.reshape(steps * rows, depth),
        w_query,
        jnp.swapaxes(adapter_down, 1, 2).reshape(adapters * rank, depth),
        adapter_up.reshape(adapters * rank, columns),
        agent_id.reshape(1, rows),
        adapter_slot.reshape(1, -1),
        cache_keys,
        cache_values,
        new_keys,
        new_values,
        lengths.reshape(1, -1),
    ).astype(bf16)


def solution(mesh):
    return jax.shard_map(
        local,
        mesh=mesh,
        in_specs=(
            P(None, ("group", "dp"), "tensor"),
            P(None, "tensor"),
            P(("group", "dp"), "tensor", None),
            P(("group", "dp"), None, "tensor"),
            P(("group", "dp")),
            P("group"),
            P(("group", "dp", "tensor"), None, None),
            P(("group", "dp", "tensor"), None, None),
            P(None, ("group", "dp", "tensor"), None),
            P(None, ("group", "dp", "tensor"), None),
            P(("group", "dp", "tensor")),
        ),
        out_specs=P(None, ("group", "dp", "tensor"), None),
        check_vma=False,
    )
```

```python
import functools

import jax
import jax.numpy as jnp
from jax import lax
from jax.experimental import pallas as pl
from jax.experimental.pallas import tpu as pltpu
from jax.sharding import PartitionSpec as P

HD = 128
KVH = 4
MESH = pl.DeviceIdType.MESH
LANES = 128
VMEM_BYTES = 62 * 1024 * 1024


def attend(steps, row_block, parts, keys_buf, values_buf, fresh_keys, fresh_values, lengths, out_ref):
    length_max = keys_buf.shape[1]
    cached = row_block * length_max
    queries = steps * row_block
    per_part = parts[0].shape[1] // HD
    group_size = len(parts) * per_part // KVH
    total = group_size * queries
    key_row = lax.broadcasted_iota(jnp.int32, (1, cached), 1) // length_max
    key_at = lax.rem(lax.broadcasted_iota(jnp.int32, (1, cached), 1), length_max)
    lane = lax.broadcasted_iota(jnp.int32, (1, row_block), 1)
    limit = jnp.zeros((1, cached), jnp.int32)
    for r in range(row_block):
        one = jnp.sum(jnp.where(lane == r, lengths, 0), axis=1, keepdims=True)
        limit = jnp.where(key_row == r, one, limit)
    key_row = jnp.where(key_at < limit, key_row, -1)
    query = lax.rem(lax.broadcasted_iota(jnp.int32, (total, 1), 0), queries)
    query_row, query_step = lax.rem(query, row_block), query // row_block
    old_valid = key_row == query_row
    fresh = lax.broadcasted_iota(jnp.int32, (1, queries), 1)
    new_valid = (lax.rem(fresh, row_block) == query_row) & (fresh // row_block <= query_step)
    contract = (((1,), (1,)), ((), ()))
    for g in range(KVH):
        cols = slice(g * HD, (g + 1) * HD)
        heads = range(g * group_size, (g + 1) * group_size)
        q = [parts[h // per_part][:, (h % per_part) * HD:(h % per_part + 1) * HD] for h in heads]
        q = (q[0] if len(q) == 1 else jnp.concatenate(q, axis=0)).astype(jnp.bfloat16)
        keys = keys_buf[:, :, cols].reshape(cached, HD)
        values = values_buf[:, :, cols].reshape(cached, HD)
        old = lax.dot_general(q, keys, contract, preferred_element_type=jnp.float32)
        new = lax.dot_general(
            q, fresh_keys[:, cols], contract, preferred_element_type=jnp.float32
        )
        old = jnp.where(old_valid, old * HD ** (-0.5), -jnp.inf)
        new = jnp.where(new_valid, new * HD ** (-0.5), -jnp.inf)
        top = jnp.maximum(
            jnp.max(old, axis=1, keepdims=True), jnp.max(new, axis=1, keepdims=True)
        )
        old, new = jnp.exp(old - top), jnp.exp(new - top)
        norm = jnp.sum(old, axis=1, keepdims=True) + jnp.sum(new, axis=1, keepdims=True)
        old, new = (old / norm).astype(jnp.bfloat16), (new / norm).astype(jnp.bfloat16)
        mixed = jnp.dot(old, values, preferred_element_type=jnp.float32)
        mixed += jnp.dot(new, fresh_values[:, cols], preferred_element_type=jnp.float32)
        for i, h in enumerate(heads):
            out_ref[:, :, h * HD:(h + 1) * HD] = (
                mixed[i * queries:(i + 1) * queries]
                .reshape(steps, row_block, HD)
                .astype(jnp.bfloat16)
            )


def rows_of(index, size):
    return pl.ds(pl.multiple_of(index * size, size), size)


def decode_kernel(
    sizes,
    x_ref,
    w_ref,
    down_ref,
    up_ref,
    agent_ref,
    slot_ref,
    keys_ref,
    values_ref,
    new_keys_ref,
    new_values_ref,
    lengths_ref,
    out_ref,
    w_parts,
    down_buf,
    x_out,
    x_in,
    low_out,
    low_in,
    low_all,
    corr_out,
    corr_in,
    delta_out,
    delta_in,
    base_out,
    base_in,
    keys_buf,
    values_buf,
    copy_sem,
    z_send,
    z_recv,
    d_send,
    d_recv,
    b_send,
    b_recv,
    c_send,
    c_recv,
    l_send,
    l_recv,
    a_send,
    a_recv,
    r_send,
    r_recv,
    e_send,
    e_recv,
    s_send,
    s_recv,
):
    n_group, n_dp, n_tensor, steps, rows, capacity, adapters, rank = sizes
    depth = w_parts.shape[1]
    n_chip_x = n_dp // 2
    chips = n_group * n_chip_x
    piece = depth // (2 * chips)
    row_block = rows // n_tensor
    per_home = steps * capacity
    items = n_dp * per_home
    low_rows = items // n_tensor

    group = lax.axis_index("group")
    dp = lax.axis_index("dp")
    tensor = lax.axis_index("tensor")
    core = lax.rem(dp, 2)
    chip = group * n_chip_x + dp // 2

    def at_chip(number, which):
        return (number // n_chip_x, lax.rem(number, n_chip_x) * 2 + which, tensor)

    sibling = (group, (dp // 2) * 2 + (1 - core), tensor)

    def remote(src, dst, send, recv, device):
        return pltpu.make_async_remote_copy(
            src_ref=src, dst_ref=dst, send_sem=send, recv_sem=recv, device_id=device,
            device_id_type=MESH,
        )

    def up_t(k):
        return lax.rem(tensor + k, n_tensor)

    def from_t(k):
        return lax.rem(tensor - k + n_tensor, n_tensor)

    def up_d(j):
        return lax.rem(dp + j, n_dp)

    def from_d(j):
        return lax.rem(dp - j + n_dp, n_dp)

    own_w = pltpu.make_async_copy(w_ref.at[rows_of(tensor, depth)], w_parts.at[0], copy_sem.at[0])
    own_down = pltpu.make_async_copy(down_ref, down_buf, copy_sem.at[1])
    own_w.start()
    own_down.start()
    own_keys = pltpu.make_async_copy(keys_ref, keys_buf, copy_sem.at[2])
    own_values = pltpu.make_async_copy(values_ref, values_buf, copy_sem.at[3])

    barrier = pltpu.get_barrier_semaphore()
    for k in range(1, n_tensor):
        pl.semaphore_signal(barrier, inc=1, device_id=(group, dp, up_t(k)), device_id_type=MESH)
    for j in range(1, n_dp):
        pl.semaphore_signal(barrier, inc=1, device_id=(group, up_d(j), tensor), device_id_type=MESH)
    for other in range(1, n_group):
        for j in range(n_dp):
            if j % 2 == 0:
                pl.semaphore_signal(
                    barrier, inc=1,
                    device_id=(lax.rem(group + other, n_group), up_d(j), tensor),
                    device_id_type=MESH,
                )
    pl.semaphore_wait(barrier, n_tensor - 1 + n_dp - 1 + (n_group - 1) * n_chip_x)

    mine = rows_of(chip * 2 + core, piece)

    def z_copy(k):
        start = up_t(k) * depth + (chip * 2 + core) * piece
        return remote(
            w_ref.at[pl.ds(pl.multiple_of(start, piece), piece)], w_parts.at[k, mine],
            z_send.at[k], z_recv.at[k], (group, dp, up_t(k)),
        )

    lax.fori_loop(1, n_tensor, lambda k, c: (z_copy(k).start(), c)[1], 0)

    agents = slot_ref.shape[1]
    width = steps * rows

    def as_column(row, count):
        diagonal = lax.broadcasted_iota(jnp.int32, (count, count), 0) == lax.broadcasted_iota(
            jnp.int32, (count, count), 1
        )
        return jnp.sum(jnp.where(diagonal, row, 0), axis=1, keepdims=True)

    agent_row, slot_row = agent_ref[...], slot_ref[...]
    agent_col, slot_col = as_column(agent_row, rows), as_column(slot_row, agents)
    agent_row = jnp.concatenate([agent_row] * steps, axis=1)
    slot_lane = jnp.sum(
        jnp.where(
            lax.broadcasted_iota(jnp.int32, (agents, width), 0) == agent_row,
            slot_col, 0,
        ),
        axis=0, keepdims=True,
    )
    slot_sub = jnp.sum(
        jnp.where(
            lax.broadcasted_iota(jnp.int32, (rows, agents), 1) == agent_col,
            slot_row, 0,
        ),
        axis=1, keepdims=True,
    )
    home_lane = slot_lane // adapters
    home_sub = slot_sub // adapters
    row_lane = lax.rem(lax.broadcasted_iota(jnp.int32, (rows, width), 1), rows)
    earlier = (home_sub == home_lane) & (
        lax.broadcasted_iota(jnp.int32, (rows, width), 0) < row_lane
    )
    place_lane = jnp.sum(earlier.astype(jnp.int32), axis=0, keepdims=True)
    step_lane = lax.broadcasted_iota(jnp.int32, (1, width), 1) // rows
    target = jnp.where(
        place_lane < capacity, (home_lane * steps + step_lane) * capacity + place_lane, items
    )
    dispatch = jnp.where(
        lax.broadcasted_iota(jnp.int32, (items, width), 0) == target, 1.0, 0.0
    )
    local_index = jnp.sum(dispatch * (slot_lane - home_lane * adapters).astype(jnp.float32),
                          axis=1, keepdims=True)
    dispatch = dispatch.astype(jnp.bfloat16)
    sent = jnp.dot(dispatch, x_ref[...], preferred_element_type=jnp.float32)
    x_out[:, :, :depth] = sent.astype(jnp.bfloat16).reshape(n_dp, per_home, depth)
    x_out[:, :, depth:] = jnp.broadcast_to(local_index, (items, LANES)).astype(
        jnp.bfloat16
    ).reshape(n_dp, per_home, LANES)

    d_copies = []
    for j in range(1, n_dp):
        d_copies.append(
            remote(x_out.at[up_d(j)], x_in.at[dp], d_send.at[j], d_recv.at[j],
                   (group, up_d(j), tensor))
        )
        d_copies[-1].start()
    x_in[dp] = x_out[dp]

    def b_copy(k, q):
        return remote(
            w_parts.at[k, mine], w_parts.at[k, mine], b_send.at[k, q], b_recv.at[k, q],
            at_chip(lax.rem(chip + q, chips), core),
        )

    def c_copy(k, q):
        part = rows_of(lax.rem(chip - q + chips, chips) * 2 + core, piece)
        return remote(
            w_parts.at[k, part], w_parts.at[k, part], c_send.at[k, q], c_recv.at[k, q], sibling
        )

    def b_arrival(k, q):
        part = rows_of(lax.rem(chip - q + chips, chips) * 2 + core, piece)
        return remote(
            w_parts.at[k, part], w_parts.at[k, part], b_send.at[k, q], b_recv.at[k, q],
            at_chip(lax.rem(chip + q, chips), core),
        )

    def c_arrival(k, q):
        part = rows_of(lax.rem(chip - q + chips, chips) * 2 + 1 - core, piece)
        return remote(
            w_parts.at[k, part], w_parts.at[k, part], c_send.at[k, q], c_recv.at[k, q], sibling
        )

    def spread(k, carry):
        z_copy(k).wait_recv()
        for q in range(1, chips):
            b_copy(k, q).start()
        c_copy(k, 0).start()
        return carry

    def forward(k, carry):
        for q in range(1, chips):
            b_arrival(k, q).wait_recv()
            c_copy(k, q).start()
        return carry

    cut = [1 + (n_tensor - 1) * i // 3 for i in range(4)]
    def project(k):
        block = jnp.dot(x_ref[...], w_parts[k], preferred_element_type=jnp.float32)
        column = from_t(k)
        for t in range(n_tensor):
            for s in range(steps):
                base_out[t, column, s * row_block:(s + 1) * row_block, :] = block[
                    s * rows + t * row_block:s * rows + (t + 1) * row_block
                ]
        for j in range(1, n_tensor):
            remote(base_out.at[up_t(j), column], base_in.at[j, column], s_send.at[j],
                   s_recv.at[j], (group, dp, up_t(j))).start()

    def project_arrived(k, carry):
        for q in range(chips):
            c_arrival(k, q).wait_recv()
        project(k)
        return carry

    own_w.wait()
    project(0)
    own_keys.start()
    own_values.start()
    lax.fori_loop(1, n_tensor, spread, 0)

    own_down.wait()
    for copy in d_copies:
        copy.wait_recv()
    arrived = x_in[...].reshape(items, depth + LANES)
    chosen = arrived[:, depth:].astype(jnp.float32)[:, :rank]
    dense = lax.dot_general(
        arrived[:, :depth], down_buf[...], (((1,), (1,)), ((), ())),
        preferred_element_type=jnp.float32,
    )
    low = jnp.zeros((items, rank), jnp.float32)
    for a in range(adapters):
        low += jnp.where(chosen == float(a), dense[:, a * rank:(a + 1) * rank], 0.0)
    low_out[...] = low.reshape(n_tensor, low_rows, rank)
    l_copies = []
    for k in range(1, n_tensor):
        l_copies.append(
            remote(low_out.at[up_t(k)], low_in.at[k], l_send.at[k], l_recv.at[k],
                   (group, dp, up_t(k)))
        )
        l_copies[-1].start()
    lax.fori_loop(cut[0], cut[1], forward, 0)
    total = low_out[tensor]
    for k in range(1, n_tensor):
        l_copies[k - 1].wait_recv()
        total += low_in[k]
    low_all[tensor] = total.astype(jnp.bfloat16)
    a_copies = []
    for k in range(1, n_tensor):
        a_copies.append(
            remote(low_all.at[tensor], low_all.at[tensor], a_send.at[k], a_recv.at[k],
                   (group, dp, up_t(k)))
        )
        a_copies[-1].start()
    for k in range(1, n_tensor):
        remote(low_all.at[from_t(k)], low_all.at[from_t(k)], a_send.at[k], a_recv.at[k],
               (group, dp, up_t(k))).wait_recv()
    low_rank = low_all[...].reshape(items, rank).astype(jnp.float32)
    spread_low = jnp.concatenate(
        [jnp.where(chosen == float(a), low_rank, 0.0) for a in range(adapters)], axis=1
    ).astype(jnp.bfloat16)
    corr = jnp.dot(spread_low, up_ref[...], preferred_element_type=jnp.float32)
    corr_out[...] = corr.astype(jnp.bfloat16).reshape(corr_out.shape)
    r_copies = []
    for j in range(1, n_dp):
        r_copies.append(
            remote(corr_out.at[up_d(j)], corr_in.at[dp], r_send.at[j], r_recv.at[j],
                   (group, up_d(j), tensor))
        )
        r_copies[-1].start()
    corr_in[dp] = corr_out[dp]
    lax.fori_loop(cut[1], cut[3], forward, 0)
    lax.fori_loop(cut[0], cut[2], project_arrived, 0)


    for copy in r_copies:
        copy.wait_recv()
    delta = lax.dot_general(
        dispatch, corr_in[...].reshape(items, corr_in.shape[2]), (((0,), (0,)), ((), ())),
        preferred_element_type=jnp.float32,
    )
    for t in range(n_tensor):
        delta_out[t] = jnp.concatenate(
            [delta[s * rows + t * row_block:s * rows + (t + 1) * row_block] for s in range(steps)],
            axis=0,
        ).astype(jnp.bfloat16)
    e_copies = []
    for k in range(1, n_tensor):
        e_copies.append(
            remote(delta_out.at[up_t(k)], delta_in.at[tensor], e_send.at[k], e_recv.at[k],
                   (group, dp, up_t(k)))
        )
        e_copies[-1].start()
    delta_in[tensor] = delta_out[tensor]

    lax.fori_loop(cut[2], cut[3], project_arrived, 0)
    own_keys.wait()
    own_values.wait()

    for copy in e_copies:
        copy.wait_recv()
    base = base_out[tensor]
    s_waits = []
    for j in range(1, n_tensor):
        s_waits.append(
            remote(base_out.at[up_t(j)], base_in.at[j], s_send.at[j], s_recv.at[j],
                   (group, dp, up_t(j)))
        )
        s_waits[-1].wait_recv()
        base += base_in[j]
    parts = [base[t] + delta_in[t].astype(jnp.float32) for t in range(n_tensor)]
    fresh_shape = (steps * row_block, new_keys_ref.shape[2])
    attend(
        steps, row_block, parts, keys_buf, values_buf,
        new_keys_ref[...].astype(jnp.float32).reshape(fresh_shape).astype(jnp.bfloat16),
        new_values_ref[...].astype(jnp.float32).reshape(fresh_shape).astype(jnp.bfloat16),
        lengths_ref[...], out_ref,
    )

    for copy in d_copies + l_copies + a_copies + r_copies + e_copies + s_waits:
        copy.wait_send()

    def drain(k, carry):
        z_copy(k).wait_send()
        for q in range(1, chips):
            b_copy(k, q).wait_send()
        for q in range(chips):
            c_copy(k, q).wait_send()
        return carry

    lax.fori_loop(1, n_tensor, drain, 0)


def local(
    x_feats,
    w_query,
    adapter_down,
    adapter_up,
    agent_id,
    adapter_slot,
    cache_keys,
    cache_values,
    new_keys,
    new_values,
    lengths,
):
    steps, rows, depth = x_feats.shape
    columns = w_query.shape[1]
    n_group, n_dp, n_tensor = (lax.axis_size(name) for name in ("group", "dp", "tensor"))
    adapters, _, rank = adapter_down.shape
    capacity = rows // 4
    row_block = rows // n_tensor
    per_home = steps * capacity
    items = n_dp * per_home
    chips = n_group * n_dp // 2
    sizes = (n_group, n_dp, n_tensor, steps, rows, capacity, adapters, rank)
    vmem = pl.BlockSpec(memory_space=pltpu.VMEM)
    hbm = pl.BlockSpec(memory_space=pl.ANY)
    bf16, f32 = jnp.bfloat16, jnp.float32
    own = steps * row_block
    dma = pltpu.SemaphoreType.DMA
    tensor_sems = [dma((n_tensor,)), dma((n_tensor,))]
    dp_sems = [dma((n_dp,)), dma((n_dp,))]
    return pl.pallas_call(
        functools.partial(decode_kernel, sizes),
        out_shape=jax.ShapeDtypeStruct((steps, row_block, n_tensor * columns), bf16),
        in_specs=[vmem, hbm, hbm, vmem, vmem, vmem, hbm, hbm, vmem, vmem, vmem],
        out_specs=vmem,
        scratch_shapes=[
            pltpu.VMEM((n_tensor, depth, columns), bf16),
            pltpu.VMEM((adapters * rank, depth), bf16),
            pltpu.VMEM((n_dp, per_home, depth + LANES), bf16),
            pltpu.VMEM((n_dp, per_home, depth + LANES), bf16),
            pltpu.VMEM((n_tensor, items // n_tensor, rank), f32),
            pltpu.VMEM((n_tensor, items // n_tensor, rank), f32),
            pltpu.VMEM((n_tensor, items // n_tensor, rank), bf16),
            pltpu.VMEM((n_dp, per_home, columns), bf16),
            pltpu.VMEM((n_dp, per_home, columns), bf16),
            pltpu.VMEM((n_tensor, own, columns), bf16),
            pltpu.VMEM((n_tensor, own, columns), bf16),
            pltpu.VMEM((n_tensor, n_tensor, own, columns), f32),
            pltpu.VMEM((n_tensor, n_tensor, own, columns), f32),
            pltpu.VMEM(cache_keys.shape, bf16),
            pltpu.VMEM(cache_values.shape, bf16),
            dma((4,)),
            *tensor_sems,
            *dp_sems,
            dma((n_tensor, chips)),
            dma((n_tensor, chips)),
            dma((n_tensor, chips)),
            dma((n_tensor, chips)),
            *tensor_sems,
            *tensor_sems,
            *dp_sems,
            *tensor_sems,
            *tensor_sems,
        ],
        compiler_params=pltpu.CompilerParams(
            collective_id=0, has_side_effects=True, vmem_limit_bytes=VMEM_BYTES
        ),
        name="decode",
    )(
        x_feats.reshape(steps * rows, depth),
        w_query,
        jnp.swapaxes(adapter_down, 1, 2).reshape(adapters * rank, depth),
        adapter_up.reshape(adapters * rank, columns),
        agent_id.reshape(1, rows),
        adapter_slot.reshape(1, -1),
        cache_keys,
        cache_values,
        new_keys,
        new_values,
        lengths.reshape(1, -1),
    )


def solution(mesh):
    return jax.shard_map(
        local,
        mesh=mesh,
        in_specs=(
            P(None, ("group", "dp"), "tensor"),
            P(None, "tensor"),
            P(("group", "dp"), "tensor", None),
            P(("group", "dp"), None, "tensor"),
            P(("group", "dp")),
            P("group"),
            P(("group", "dp", "tensor"), None, None),
            P(("group", "dp", "tensor"), None, None),
            P(None, ("group", "dp", "tensor"), None),
            P(None, ("group", "dp", "tensor"), None),
            P(("group", "dp", "tensor")),
        ),
        out_specs=P(None, ("group", "dp", "tensor"), None),
        check_vma=False,
    )
```

```python
import functools

import jax
import jax.numpy as jnp
from jax import lax
from jax.experimental import pallas as pl
from jax.experimental.pallas import tpu as pltpu
from jax.sharding import PartitionSpec as P

HD = 128
KVH = 4
MESH = pl.DeviceIdType.MESH
LANES = 128
VMEM_BYTES = 62 * 1024 * 1024


def attend(steps, row_block, parts, keys_buf, values_buf, fresh_keys, fresh_values, lengths, out_ref):
    length_max = keys_buf.shape[1]
    cached = row_block * length_max
    queries = steps * row_block
    per_part = parts[0].shape[1] // HD
    group_size = len(parts) * per_part // KVH
    total = group_size * queries
    key_row = lax.broadcasted_iota(jnp.int32, (1, cached), 1) // length_max
    key_at = lax.rem(lax.broadcasted_iota(jnp.int32, (1, cached), 1), length_max)
    lane = lax.broadcasted_iota(jnp.int32, (1, row_block), 1)
    limit = jnp.zeros((1, cached), jnp.int32)
    for r in range(row_block):
        one = jnp.sum(jnp.where(lane == r, lengths, 0), axis=1, keepdims=True)
        limit = jnp.where(key_row == r, one, limit)
    key_row = jnp.where(key_at < limit, key_row, -1)
    query = lax.rem(lax.broadcasted_iota(jnp.int32, (total, 1), 0), queries)
    query_row, query_step = lax.rem(query, row_block), query // row_block
    old_valid = key_row == query_row
    fresh = lax.broadcasted_iota(jnp.int32, (1, queries), 1)
    new_valid = (lax.rem(fresh, row_block) == query_row) & (fresh // row_block <= query_step)
    contract = (((1,), (1,)), ((), ()))
    for g in range(KVH):
        cols = slice(g * HD, (g + 1) * HD)
        heads = range(g * group_size, (g + 1) * group_size)
        q = [parts[h // per_part][:, (h % per_part) * HD:(h % per_part + 1) * HD] for h in heads]
        q = (q[0] if len(q) == 1 else jnp.concatenate(q, axis=0)).astype(jnp.bfloat16)
        keys = keys_buf[:, :, cols].reshape(cached, HD)
        values = values_buf[:, :, cols].reshape(cached, HD)
        old = lax.dot_general(q, keys, contract, preferred_element_type=jnp.float32)
        new = lax.dot_general(
            q, fresh_keys[:, cols], contract, preferred_element_type=jnp.float32
        )
        old = jnp.where(old_valid, old * HD ** (-0.5), -jnp.inf)
        new = jnp.where(new_valid, new * HD ** (-0.5), -jnp.inf)
        top = jnp.maximum(
            jnp.max(old, axis=1, keepdims=True), jnp.max(new, axis=1, keepdims=True)
        )
        old, new = jnp.exp(old - top), jnp.exp(new - top)
        norm = jnp.sum(old, axis=1, keepdims=True) + jnp.sum(new, axis=1, keepdims=True)
        old, new = (old / norm).astype(jnp.bfloat16), (new / norm).astype(jnp.bfloat16)
        mixed = jnp.dot(old, values, preferred_element_type=jnp.float32)
        mixed += jnp.dot(new, fresh_values[:, cols], preferred_element_type=jnp.float32)
        for i, h in enumerate(heads):
            out_ref[:, :, h * HD:(h + 1) * HD] = (
                mixed[i * queries:(i + 1) * queries]
                .reshape(steps, row_block, HD)
                .astype(jnp.bfloat16)
            )


def rows_of(index, size):
    return pl.ds(pl.multiple_of(index * size, size), size)


def decode_kernel(
    sizes,
    x_ref,
    w_ref,
    down_ref,
    up_ref,
    agent_ref,
    slot_ref,
    keys_ref,
    values_ref,
    new_keys_ref,
    new_values_ref,
    lengths_ref,
    out_ref,
    w_parts,
    down_buf,
    x_out,
    x_in,
    low_out,
    low_in,
    low_all,
    corr_out,
    corr_in,
    delta_out,
    delta_in,
    base_out,
    base_in,
    keys_buf,
    values_buf,
    copy_sem,
    z_send,
    z_recv,
    d_send,
    d_recv,
    b_send,
    b_recv,
    c_send,
    c_recv,
    l_send,
    l_recv,
    a_send,
    a_recv,
    r_send,
    r_recv,
    e_send,
    e_recv,
    s_send,
    s_recv,
):
    n_group, n_dp, n_tensor, steps, rows, capacity, adapters, rank = sizes
    depth = w_parts.shape[1]
    n_chip_x = n_dp // 2
    chips = n_group * n_chip_x
    piece = depth // (2 * chips)
    row_block = rows // n_tensor
    per_home = steps * capacity
    items = n_dp * per_home
    low_rows = items // n_tensor

    group = lax.axis_index("group")
    dp = lax.axis_index("dp")
    tensor = lax.axis_index("tensor")
    core = lax.rem(dp, 2)
    chip = group * n_chip_x + dp // 2

    def at_chip(number, which):
        return (number // n_chip_x, lax.rem(number, n_chip_x) * 2 + which, tensor)

    sibling = (group, (dp // 2) * 2 + (1 - core), tensor)

    def remote(src, dst, send, recv, device):
        return pltpu.make_async_remote_copy(
            src_ref=src, dst_ref=dst, send_sem=send, recv_sem=recv, device_id=device,
            device_id_type=MESH,
        )

    def up_t(k):
        return lax.rem(tensor + k, n_tensor)

    def from_t(k):
        return lax.rem(tensor - k + n_tensor, n_tensor)

    def up_d(j):
        return lax.rem(dp + j, n_dp)

    def from_d(j):
        return lax.rem(dp - j + n_dp, n_dp)

    own_w = pltpu.make_async_copy(w_ref.at[rows_of(tensor, depth)], w_parts.at[0], copy_sem.at[0])
    own_down = pltpu.make_async_copy(down_ref, down_buf, copy_sem.at[1])
    own_w.start()
    own_down.start()
    own_keys = pltpu.make_async_copy(keys_ref, keys_buf, copy_sem.at[2])
    own_values = pltpu.make_async_copy(values_ref, values_buf, copy_sem.at[3])

    barrier = pltpu.get_barrier_semaphore()
    for k in range(1, n_tensor):
        pl.semaphore_signal(barrier, inc=1, device_id=(group, dp, up_t(k)), device_id_type=MESH)
    for j in range(1, n_dp):
        pl.semaphore_signal(barrier, inc=1, device_id=(group, up_d(j), tensor), device_id_type=MESH)
    for other in range(1, n_group):
        for j in range(n_dp):
            if j % 2 == 0:
                pl.semaphore_signal(
                    barrier, inc=1,
                    device_id=(lax.rem(group + other, n_group), up_d(j), tensor),
                    device_id_type=MESH,
                )
    pl.semaphore_wait(barrier, n_tensor - 1 + n_dp - 1 + (n_group - 1) * n_chip_x)

    mine = rows_of(chip * 2 + core, piece)

    def z_copy(k):
        start = up_t(k) * depth + (chip * 2 + core) * piece
        return remote(
            w_ref.at[pl.ds(pl.multiple_of(start, piece), piece)], w_parts.at[k, mine],
            z_send.at[k], z_recv.at[k], (group, dp, up_t(k)),
        )

    lax.fori_loop(1, n_tensor, lambda k, c: (z_copy(k).start(), c)[1], 0)

    agents = slot_ref.shape[1]
    width = steps * rows

    def as_column(row, count):
        diagonal = lax.broadcasted_iota(jnp.int32, (count, count), 0) == lax.broadcasted_iota(
            jnp.int32, (count, count), 1
        )
        return jnp.sum(jnp.where(diagonal, row, 0), axis=1, keepdims=True)

    agent_row, slot_row = agent_ref[...], slot_ref[...]
    agent_col, slot_col = as_column(agent_row, rows), as_column(slot_row, agents)
    agent_row = jnp.concatenate([agent_row] * steps, axis=1)
    slot_lane = jnp.sum(
        jnp.where(
            lax.broadcasted_iota(jnp.int32, (agents, width), 0) == agent_row,
            slot_col, 0,
        ),
        axis=0, keepdims=True,
    )
    slot_sub = jnp.sum(
        jnp.where(
            lax.broadcasted_iota(jnp.int32, (rows, agents), 1) == agent_col,
            slot_row, 0,
        ),
        axis=1, keepdims=True,
    )
    home_lane = slot_lane // adapters
    home_sub = slot_sub // adapters
    row_lane = lax.rem(lax.broadcasted_iota(jnp.int32, (rows, width), 1), rows)
    earlier = (home_sub == home_lane) & (
        lax.broadcasted_iota(jnp.int32, (rows, width), 0) < row_lane
    )
    place_lane = jnp.sum(earlier.astype(jnp.int32), axis=0, keepdims=True)
    step_lane = lax.broadcasted_iota(jnp.int32, (1, width), 1) // rows
    target = jnp.where(
        place_lane < capacity, (home_lane * steps + step_lane) * capacity + place_lane, items
    )
    dispatch = jnp.where(
        lax.broadcasted_iota(jnp.int32, (items, width), 0) == target, 1.0, 0.0
    )
    local_index = jnp.sum(dispatch * (slot_lane - home_lane * adapters).astype(jnp.float32),
                          axis=1, keepdims=True)
    dispatch = dispatch.astype(jnp.bfloat16)
    sent = jnp.dot(dispatch, x_ref[...], preferred_element_type=jnp.float32)
    x_out[:, :, :depth] = sent.astype(jnp.bfloat16).reshape(n_dp, per_home, depth)
    x_out[:, :, depth:] = jnp.broadcast_to(local_index, (items, LANES)).astype(
        jnp.bfloat16
    ).reshape(n_dp, per_home, LANES)

    d_copies = []
    for j in range(1, n_dp):
        d_copies.append(
            remote(x_out.at[up_d(j)], x_in.at[dp], d_send.at[j], d_recv.at[j],
                   (group, up_d(j), tensor))
        )
        d_copies[-1].start()
    x_in[dp] = x_out[dp]

    def b_copy(k, q):
        return remote(
            w_parts.at[k, mine], w_parts.at[k, mine], b_send.at[k, q], b_recv.at[k, q],
            at_chip(lax.rem(chip + q, chips), core),
        )

    def c_copy(k, q):
        part = rows_of(lax.rem(chip - q + chips, chips) * 2 + core, piece)
        return remote(
            w_parts.at[k, part], w_parts.at[k, part], c_send.at[k, q], c_recv.at[k, q], sibling
        )

    def b_arrival(k, q):
        part = rows_of(lax.rem(chip - q + chips, chips) * 2 + core, piece)
        return remote(
            w_parts.at[k, part], w_parts.at[k, part], b_send.at[k, q], b_recv.at[k, q],
            at_chip(lax.rem(chip + q, chips), core),
        )

    def c_arrival(k, q):
        part = rows_of(lax.rem(chip - q + chips, chips) * 2 + 1 - core, piece)
        return remote(
            w_parts.at[k, part], w_parts.at[k, part], c_send.at[k, q], c_recv.at[k, q], sibling
        )

    def spread(k, carry):
        z_copy(k).wait_recv()
        for q in range(1, chips):
            b_copy(k, q).start()
        c_copy(k, 0).start()
        return carry

    def forward(k, carry):
        for q in range(1, chips):
            b_arrival(k, q).wait_recv()
            c_copy(k, q).start()
        return carry

    cut = [1 + (n_tensor - 1) * i // 3 for i in range(4)]
    def project(k):
        block = jnp.dot(x_ref[...], w_parts[k], preferred_element_type=jnp.float32)
        column = from_t(k)
        for t in range(n_tensor):
            for s in range(steps):
                base_out[t, column, s * row_block:(s + 1) * row_block, :] = block[
                    s * rows + t * row_block:s * rows + (t + 1) * row_block
                ]
        for j in range(1, n_tensor):
            remote(base_out.at[up_t(j), column], base_in.at[j, column], s_send.at[j],
                   s_recv.at[j], (group, dp, up_t(j))).start()

    def project_arrived(k, carry):
        for q in range(chips):
            c_arrival(k, q).wait_recv()
        project(k)
        return carry

    own_w.wait()
    project(0)
    own_keys.start()
    own_values.start()
    lax.fori_loop(cut[0], cut[2], spread, 0)

    own_down.wait()
    for copy in d_copies:
        copy.wait_recv()
    arrived = x_in[...].reshape(items, depth + LANES)
    chosen = arrived[:, depth:].astype(jnp.float32)[:, :rank]
    dense = lax.dot_general(
        arrived[:, :depth], down_buf[...], (((1,), (1,)), ((), ())),
        preferred_element_type=jnp.float32,
    )
    low = jnp.zeros((items, rank), jnp.float32)
    for a in range(adapters):
        low += jnp.where(chosen == float(a), dense[:, a * rank:(a + 1) * rank], 0.0)
    low_out[...] = low.reshape(n_tensor, low_rows, rank)
    l_copies = []
    for k in range(1, n_tensor):
        l_copies.append(
            remote(low_out.at[up_t(k)], low_in.at[k], l_send.at[k], l_recv.at[k],
                   (group, dp, up_t(k)))
        )
        l_copies[-1].start()
    lax.fori_loop(cut[2], cut[3], spread, 0)
    total = low_out[tensor]
    for k in range(1, n_tensor):
        l_copies[k - 1].wait_recv()
        total += low_in[k]
    low_all[tensor] = total.astype(jnp.bfloat16)
    a_copies = []
    for k in range(1, n_tensor):
        a_copies.append(
            remote(low_all.at[tensor], low_all.at[tensor], a_send.at[k], a_recv.at[k],
                   (group, dp, up_t(k)))
        )
        a_copies[-1].start()
    lax.fori_loop(cut[0], cut[1], forward, 0)
    for k in range(1, n_tensor):
        remote(low_all.at[from_t(k)], low_all.at[from_t(k)], a_send.at[k], a_recv.at[k],
               (group, dp, up_t(k))).wait_recv()
    low_rank = low_all[...].reshape(items, rank).astype(jnp.float32)
    spread_low = jnp.concatenate(
        [jnp.where(chosen == float(a), low_rank, 0.0) for a in range(adapters)], axis=1
    ).astype(jnp.bfloat16)
    corr = jnp.dot(spread_low, up_ref[...], preferred_element_type=jnp.float32)
    corr_out[...] = corr.astype(jnp.bfloat16).reshape(corr_out.shape)
    r_copies = []
    for j in range(1, n_dp):
        r_copies.append(
            remote(corr_out.at[up_d(j)], corr_in.at[dp], r_send.at[j], r_recv.at[j],
                   (group, up_d(j), tensor))
        )
        r_copies[-1].start()
    corr_in[dp] = corr_out[dp]
    lax.fori_loop(cut[1], cut[3], forward, 0)
    lax.fori_loop(cut[0], cut[2], project_arrived, 0)


    for copy in r_copies:
        copy.wait_recv()
    delta = lax.dot_general(
        dispatch, corr_in[...].reshape(items, corr_in.shape[2]), (((0,), (0,)), ((), ())),
        preferred_element_type=jnp.float32,
    )
    for t in range(n_tensor):
        delta_out[t] = jnp.concatenate(
            [delta[s * rows + t * row_block:s * rows + (t + 1) * row_block] for s in range(steps)],
            axis=0,
        ).astype(jnp.bfloat16)
    e_copies = []
    for k in range(1, n_tensor):
        e_copies.append(
            remote(delta_out.at[up_t(k)], delta_in.at[tensor], e_send.at[k], e_recv.at[k],
                   (group, dp, up_t(k)))
        )
        e_copies[-1].start()
    delta_in[tensor] = delta_out[tensor]

    lax.fori_loop(cut[2], cut[3], project_arrived, 0)
    own_keys.wait()
    own_values.wait()

    for copy in e_copies:
        copy.wait_recv()
    base = base_out[tensor]
    s_waits = []
    for j in range(1, n_tensor):
        s_waits.append(
            remote(base_out.at[up_t(j)], base_in.at[j], s_send.at[j], s_recv.at[j],
                   (group, dp, up_t(j)))
        )
        s_waits[-1].wait_recv()
        base += base_in[j]
    parts = [base[t] + delta_in[t].astype(jnp.float32) for t in range(n_tensor)]
    fresh_shape = (steps * row_block, new_keys_ref.shape[2])
    attend(
        steps, row_block, parts, keys_buf, values_buf,
        new_keys_ref[...].astype(jnp.float32).reshape(fresh_shape).astype(jnp.bfloat16),
        new_values_ref[...].astype(jnp.float32).reshape(fresh_shape).astype(jnp.bfloat16),
        lengths_ref[...], out_ref,
    )

    for copy in d_copies + l_copies + a_copies + r_copies + e_copies + s_waits:
        copy.wait_send()

    def drain(k, carry):
        z_copy(k).wait_send()
        for q in range(1, chips):
            b_copy(k, q).wait_send()
        for q in range(chips):
            c_copy(k, q).wait_send()
        return carry

    lax.fori_loop(1, n_tensor, drain, 0)


def local(
    x_feats,
    w_query,
    adapter_down,
    adapter_up,
    agent_id,
    adapter_slot,
    cache_keys,
    cache_values,
    new_keys,
    new_values,
    lengths,
):
    steps, rows, depth = x_feats.shape
    columns = w_query.shape[1]
    n_group, n_dp, n_tensor = (lax.axis_size(name) for name in ("group", "dp", "tensor"))
    adapters, _, rank = adapter_down.shape
    capacity = rows // 4
    row_block = rows // n_tensor
    per_home = steps * capacity
    items = n_dp * per_home
    chips = n_group * n_dp // 2
    sizes = (n_group, n_dp, n_tensor, steps, rows, capacity, adapters, rank)
    vmem = pl.BlockSpec(memory_space=pltpu.VMEM)
    hbm = pl.BlockSpec(memory_space=pl.ANY)
    bf16, f32 = jnp.bfloat16, jnp.float32
    own = steps * row_block
    dma = pltpu.SemaphoreType.DMA
    tensor_sems = [dma((n_tensor,)), dma((n_tensor,))]
    dp_sems = [dma((n_dp,)), dma((n_dp,))]
    return pl.pallas_call(
        functools.partial(decode_kernel, sizes),
        out_shape=jax.ShapeDtypeStruct((steps, row_block, n_tensor * columns), bf16),
        in_specs=[vmem, hbm, hbm, vmem, vmem, vmem, hbm, hbm, vmem, vmem, vmem],
        out_specs=vmem,
        scratch_shapes=[
            pltpu.VMEM((n_tensor, depth, columns), bf16),
            pltpu.VMEM((adapters * rank, depth), bf16),
            pltpu.VMEM((n_dp, per_home, depth + LANES), bf16),
            pltpu.VMEM((n_dp, per_home, depth + LANES), bf16),
            pltpu.VMEM((n_tensor, items // n_tensor, rank), f32),
            pltpu.VMEM((n_tensor, items // n_tensor, rank), f32),
            pltpu.VMEM((n_tensor, items // n_tensor, rank), bf16),
            pltpu.VMEM((n_dp, per_home, columns), bf16),
            pltpu.VMEM((n_dp, per_home, columns), bf16),
            pltpu.VMEM((n_tensor, own, columns), bf16),
            pltpu.VMEM((n_tensor, own, columns), bf16),
            pltpu.VMEM((n_tensor, n_tensor, own, columns), f32),
            pltpu.VMEM((n_tensor, n_tensor, own, columns), f32),
            pltpu.VMEM(cache_keys.shape, bf16),
            pltpu.VMEM(cache_values.shape, bf16),
            dma((4,)),
            *tensor_sems,
            *dp_sems,
            dma((n_tensor, chips)),
            dma((n_tensor, chips)),
            dma((n_tensor, chips)),
            dma((n_tensor, chips)),
            *tensor_sems,
            *tensor_sems,
            *dp_sems,
            *tensor_sems,
            *tensor_sems,
        ],
        compiler_params=pltpu.CompilerParams(
            collective_id=0, has_side_effects=True, vmem_limit_bytes=VMEM_BYTES
        ),
        name="decode",
    )(
        x_feats.reshape(steps * rows, depth),
        w_query,
        jnp.swapaxes(adapter_down, 1, 2).reshape(adapters * rank, depth),
        adapter_up.reshape(adapters * rank, columns),
        agent_id.reshape(1, rows),
        adapter_slot.reshape(1, -1),
        cache_keys,
        cache_values,
        new_keys,
        new_values,
        lengths.reshape(1, -1),
    )


def solution(mesh):
    return jax.shard_map(
        local,
        mesh=mesh,
        in_specs=(
            P(None, ("group", "dp"), "tensor"),
            P(None, "tensor"),
            P(("group", "dp"), "tensor", None),
            P(("group", "dp"), None, "tensor"),
            P(("group", "dp")),
            P("group"),
            P(("group", "dp", "tensor"), None, None),
            P(("group", "dp", "tensor"), None, None),
            P(None, ("group", "dp", "tensor"), None),
            P(None, ("group", "dp", "tensor"), None),
            P(("group", "dp", "tensor")),
        ),
        out_specs=P(None, ("group", "dp", "tensor"), None),
        check_vma=False,
    )
```
